128 devices in a mesh: sec: 8 (over z, x_lo), tp: 16 (over x_hi, y, core).
Axes of the slice: x: 4 (x_hi: 2, x_lo: 2; x = x_hi * 2 + x_lo), y: 4, z: 4, core: 2. Of those that a mesh axis runs over, the one named last changes fastest.
Arguments:
- rollout: bfloat16 [16384, 8192], P('sec', 'tp'), may hold values from -96 to 96
- lengths: int32 [8, 8], P('sec'), may hold values from 1 to 256, as said below
- target: int32 [8, 8], P('sec'), may hold values from 0 to 7, as said below
- w_query: bfloat16 [8, 8192, 8192], P('sec', None, 'tp'), may hold values from -0.0625 to 0.0625
- w_keyval: bfloat16 [8, 8192, 2048], P('sec', None, 'tp'), may hold values from -0.0625 to 0.0625
- w_out: bfloat16 [8, 8192, 8192], P('sec', 'tp'), may hold values from -0.0625 to 0.0625
Outputs:
- attended: bfloat16 [8192, 8192], P('sec', 'tp')
The draws below stay inside these ranges and needn't reach their ends.
Inputs may be any that keep to these rules, and one draw needn't show every extreme that they name: `lengths`: rollout group s holds its responses one after another from the first row of its block in the order of r; the rest of the block is not read. Every response holds at most 256 tokens and some response exactly 256. The responses that go to one section group hold at most 1024 tokens together, and some section group exactly 1024. `target`: every rollout group sends exactly one response to each section group.
All inputs are finite; a program needn't handle non-finite values.
Results may differ from the reference program's by a relative error of at most 0.012.
The reference program's roundings to bfloat16 on the way count: a program that leaves them out, or rounds other values in their place, can miss the bound.
Values may be sent and summed in bfloat16 or wider, within the bound.
No kernel may reach another device: no remote copies, remote signals or barrier semaphores. Data moves between devices by JAX's collectives and lax.ppermute only.
A program may use at most 128 MiB of HBM per device.

```python
import math
import jax
import jax.numpy as jnp
from jax import lax

D = 8192
HQ = 64
KVH = 8
HD = 128
CAP = 1024
ROLL = 2048
SLOT = 256
N_SEC = 8


def one_order(one_key):
    return jax.random.permutation(one_key, N_SEC)


def plan(key):
    key_fill, key_busy, key_jitter, key_spot, key_order = jax.random.split(key, 5)
    section_ids = jnp.arange(N_SEC, dtype=jnp.int32)
    fillings = jax.random.randint(key_fill, (N_SEC,), CAP // 8, CAP // 2 + 1)
    busiest = jax.random.randint(key_busy, (), 0, N_SEC)
    fillings = jnp.where(section_ids == busiest, CAP, fillings)
    leading = jnp.where(section_ids == busiest, SLOT, fillings // N_SEC)
    remainder = fillings - leading
    base_len = remainder // (N_SEC - 1)
    jitter = jax.random.randint(key_jitter, (N_SEC, N_SEC - 1), 0, (base_len // 2 + 1)[:, None])
    pieces = base_len[:, None] + jitter - jnp.roll(jitter, 1, axis=1)
    column_ids = jnp.arange(N_SEC - 1, dtype=jnp.int32)
    pieces = pieces + jnp.where(column_ids[None, :] == 0, (remainder - (N_SEC - 1) * base_len)[:, None], 0)
    spot_idx = jax.random.randint(key_spot, (N_SEC, 1), 0, N_SEC)
    source_ids = jnp.broadcast_to(section_ids[None, :], (N_SEC, N_SEC))
    moved_ids = jnp.clip(source_ids - (source_ids > spot_idx).astype(jnp.int32), 0, N_SEC - 2)
    spread = jnp.take_along_axis(pieces, moved_ids, axis=1)
    per_target = jnp.where(source_ids == spot_idx, leading[:, None], spread)
    order_keys = jax.random.split(key_order, N_SEC)
    target = jax.vmap(one_order)(order_keys).astype(jnp.int32)
    lengths = jnp.take_along_axis(per_target.T, target, axis=1)
    return (lengths.astype(jnp.int32), target)


def draw_lengths(key, part):
    return plan(key)[0]


def draw_target(key, part):
    return plan(key)[1]


def draw_rollout(key, part):
    key = jax.random.fold_in(key, 7)
    key_values = jax.random.fold_in(key, 2)
    full_shape = (N_SEC * ROLL, D)
    values = jax.random.normal(key_values, full_shape, jnp.float32)
    return jnp.clip(values, -96.0, 96.0).astype(jnp.bfloat16)


def level_of(stream_key, shape, shards, smallest, top_value):
    def one(dim, parts):
        heights = jax.random.uniform(jax.random.fold_in(jax.random.fold_in(stream_key, 6), dim), (parts,), jnp.float32, smallest / len(shards), top_value / len(shards))
        return jnp.repeat(jnp.exp(heights), shape[dim] // parts).reshape((-1,) + (1,) * (len(shape) - dim - 1))

    gain = one(*shards[0])
    for cut in shards[1:]:
        gain = gain * one(*cut)
    return gain


def centred(own_key, dims, width, reach, cuts=(), kind=jnp.bfloat16):
    loudness = level_of(own_key, dims, cuts, -0.22, 0.18) if cuts else 1.0
    drawn = jax.random.normal(own_key, dims, jnp.float32) * width * loudness
    return jnp.minimum(jnp.maximum(drawn, -reach), reach).astype(kind)


def setup_inputs(seed: int = 0) -> dict:
    splits = jax.random.split(jax.random.key(seed), 7)
    return {
        "rollout": draw_rollout(jax.random.fold_in(splits[6], 71), 0),
        "lengths": draw_lengths(jax.random.fold_in(splits[6], 71), 0),
        "target": draw_target(jax.random.fold_in(splits[6], 71), 0),
        "w_query": centred(splits[3], (N_SEC, D, HQ * HD), D ** -0.5, 0.0625, ((0, 8), (2, 16))),
        "w_keyval": centred(splits[4], (N_SEC, D, KVH * 2 * HD), D ** -0.5, 0.0625, ((0, 8), (2, 16))),
        "w_out": centred(splits[5], (N_SEC, HQ * HD, D), (HQ * HD) ** -0.5, 0.0625, ((0, 8), (1, 16))),
    }


rope_base = 500000.0

def rotary(values, position, pair_ids, head_dim, keep):
    frequency = jnp.exp(pair_ids.astype(jnp.float32) * (-2.0 * math.log(rope_base) / head_dim))
    angles = position.astype(jnp.float32)[:, None] * frequency[None, :]
    cosine = jnp.cos(angles)
    sine_part = jnp.sin(angles)
    paired = values.reshape(values.shape[0], -1, 2)
    swapped = jnp.stack([-paired[:, :, 1], paired[:, :, 0]], axis=2).reshape(values.shape)
    turned = values * cosine + swapped * sine_part
    return jnp.where(keep[None, :], turned, values)

def packing(counts):
    end_rows = jnp.cumsum(counts)
    offsets = end_rows - counts
    row_ids = jnp.arange(CAP, dtype=jnp.int32)
    segment = lax.optimization_barrier(jnp.sum((end_rows[None, :] <= row_ids[:, None]).astype(jnp.int32), axis=1))
    filled = row_ids < end_rows[-1]
    segment = jnp.minimum(segment, counts.shape[0] - 1).astype(jnp.int32)
    position = (row_ids - offsets[segment]).astype(jnp.int32)
    return (segment, position, filled)

def attend(q_head, k_head, v_head, allowed):
    scores = jnp.dot(q_head, k_head.T, preferred_element_type=jnp.float32) / math.sqrt(HD)
    scores = jnp.where(allowed, scores, jnp.float32(-1e+30))
    row_max = lax.optimization_barrier(jnp.max(scores, axis=1, keepdims=True))
    shifted = jnp.exp(scores - row_max)
    weights = (shifted / lax.optimization_barrier(jnp.sum(shifted, axis=1, keepdims=True))).astype(jnp.bfloat16)
    return jnp.dot(weights, v_head, preferred_element_type=jnp.float32)

def reference(rollout, lengths, target, w_query, w_keyval, w_out):
    sections = lengths.shape[0]
    group_size = HQ // KVH
    before = jnp.cumsum(lengths, axis=1) - lengths
    row_ids = jnp.arange(CAP, dtype=jnp.int32)
    blocks = []
    for section in range(sections):
        chosen = target == section
        counts = lax.optimization_barrier(jnp.sum(jnp.where(chosen, lengths, 0), axis=1)).astype(jnp.int32)
        starts = lax.optimization_barrier(jnp.sum(jnp.where(chosen, before, 0), axis=1)).astype(jnp.int32)
        segment, position, filled = packing(counts)
        source_row = segment * ROLL + starts[segment] + position
        source_row = jnp.where(filled, source_row, 0).astype(jnp.int32)
        packed = jnp.where(filled[:, None], rollout[source_row], jnp.zeros((), rollout.dtype))
        query = jnp.dot(packed, w_query[section], preferred_element_type=jnp.float32)
        query_cols = jnp.arange(HQ * HD, dtype=jnp.int32)
        query = rotary(query, position, query_cols % HD // 2, HD, query_cols >= 0).astype(jnp.bfloat16)
        keyval = jnp.dot(packed, w_keyval[section], preferred_element_type=jnp.float32)
        keyval_cols = jnp.arange(KVH * 2 * HD, dtype=jnp.int32)
        keyval_pairs = keyval_cols // (2 * KVH) % (HD // 2)
        keyval = rotary(keyval, position, keyval_pairs, HD, keyval_cols < KVH * HD).astype(jnp.bfloat16)
        keyval_split = keyval.reshape(CAP, 2, HD // 2, KVH, 2)
        allowed = (segment[:, None] == segment[None, :]) & (row_ids[None, :] <= row_ids[:, None])

        def one_head(head_id):
            q_head = lax.dynamic_slice_in_dim(query, (head_id * HD).astype(jnp.int32), HD, 1)
            kv_index = (head_id // group_size).astype(jnp.int32)
            picked = lax.dynamic_index_in_dim(keyval_split, kv_index, 3, keepdims=False)
            k_head = picked[:, 0].reshape(CAP, HD)
            v_head = picked[:, 1].reshape(CAP, HD)
            return attend(q_head, k_head, v_head, allowed)
        head_rows = lax.map(one_head, jnp.arange(HQ, dtype=jnp.int32))
        head_rows = jnp.where(filled[None, :, None], head_rows, jnp.float32(0.0)).astype(jnp.bfloat16)
        head_rows = head_rows.transpose(1, 0, 2).reshape(CAP, HQ * HD)
        blocks.append(jnp.dot(head_rows, w_out[section], preferred_element_type=jnp.float32).astype(jnp.bfloat16))
    return jnp.concatenate(blocks, axis=0)
```

```python
import functools
import math

import jax
import jax.numpy as jnp
from jax import lax
from jax.experimental import pallas as pl
from jax.experimental.pallas import tpu as pltpu
from jax.sharding import PartitionSpec as P

HQ = 64
KVH = 8
HD = 128
CAP = 1024
SLOT = 256
ALIGN = 16
SENT = SLOT + ALIGN
TILE = 256
BLOCK = 512
rope_base = 500000.0
BF = jnp.bfloat16
F32 = jnp.float32


def params(mib):
    return pltpu.CompilerParams(vmem_limit_bytes=mib * 1024 * 1024)


def permutation(move):
    pairs = []
    for t in range(16):
        x, y, c = move(t // 8, t // 2 % 4, t % 2)
        pairs.append((t, x % 2 * 8 + y % 4 * 2 + c % 2))
    return pairs


TO_CORE = permutation(lambda x, y, c: (x, y, c + 1))
TO_X = permutation(lambda x, y, c: (x + 1, y, c))
TO_Y = permutation(lambda x, y, c: (x, y + 1 - 2 * c, c))


def send(value, pairs):
    return lax.ppermute(value, "tp", pairs)


def cut_kernel(start_ref, rollout_ref, first_ref, second_ref, sems):
    width = first_ref.shape[2]
    copies = []
    for part, out in enumerate((first_ref, second_ref)):
        for d in range(8):
            row = pl.multiple_of(start_ref[d], ALIGN)
            copies.append(
                pltpu.make_async_copy(
                    rollout_ref.at[pl.ds(row, SENT), pl.ds(part * width, width)],
                    out.at[d],
                    sems.at[part * 8 + d],
                )
            )
    for copy in copies:
        copy.start()
    for copy in copies:
        copy.wait()


def cut(rollout, starts):
    width = rollout.shape[1] // 2
    shape = jax.ShapeDtypeStruct((8, SENT, width), BF)
    return pl.pallas_call(
        cut_kernel,
        out_shape=(shape, shape),
        grid_spec=pltpu.PrefetchScalarGridSpec(
            num_scalar_prefetch=1,
            grid=(1,),
            in_specs=[pl.BlockSpec(memory_space=pl.ANY)],
            out_specs=[pl.BlockSpec(memory_space=pl.ANY)] * 2,
            scratch_shapes=[pltpu.SemaphoreType.DMA((16,))],
        ),
        cost_estimate=pl.CostEstimate(flops=0, bytes_accessed=8 << 20, transcendentals=0),
        name="cut",
    )(starts, rollout)


def pack_kernel(plan_ref, arrived_ref, packed_ref):
    rows = pl.program_id(0) * TILE + lax.broadcasted_iota(jnp.int32, (TILE, 1), 0)
    source = jnp.full((TILE, 1), -1, jnp.int32)
    for s in range(8):
        inside = (rows >= plan_ref[0, s]) & (rows < plan_ref[1, s])
        source = jnp.where(inside, rows + plan_ref[2, s], source)
    slots = lax.broadcasted_iota(jnp.int32, (TILE, arrived_ref.shape[0]), 1)
    picked = jnp.where(slots == source, 1.0, 0.0).astype(BF)
    packed_ref[...] = jnp.dot(
        picked, arrived_ref[...], preferred_element_type=F32
    ).astype(BF)


def pack(arrived, plan):
    slots, width = arrived.shape
    return pl.pallas_call(
        pack_kernel,
        out_shape=jax.ShapeDtypeStruct((CAP, width), BF),
        grid_spec=pltpu.PrefetchScalarGridSpec(
            num_scalar_prefetch=1,
            grid=(CAP // TILE,),
            in_specs=[pl.BlockSpec((slots, width), lambda i, p: (0, 0))],
            out_specs=pl.BlockSpec((TILE, width), lambda i, p: (i, 0)),
        ),
        compiler_params=params(32),
        cost_estimate=pl.CostEstimate(
            flops=2 * CAP * slots * width, bytes_accessed=2 << 20, transcendentals=0
        ),
        name="pack",
    )(plan, arrived)


def swap_members(values):
    lanes = lax.broadcasted_iota(jnp.int32, values.shape, 1)
    return jnp.where(
        lanes % 2 == 0, pltpu.roll(values, HD - 1, 1), pltpu.roll(values, 1, 1)
    )


def project_kernel(counts, has_total, last, *refs):
    refs = list(refs)
    refs.pop(0)
    pieces = [refs.pop(0) for _ in counts]
    n = sum(counts)
    query_w = [refs.pop(0) for _ in range(n)]
    keyval_w = [refs.pop(0) for _ in range(n)]
    total_refs = [refs.pop(0) for _ in range(2)] if has_total else None
    tables = [refs.pop(0) for _ in range(4)] if last else None
    query_out, keyval_out = refs
    query = total_refs[0][...] if has_total else None
    keyval = total_refs[1][...] if has_total else None
    k = 0
    for ref, count in zip(pieces, counts):
        for j in range(count):
            left = ref[j]
            q_term = jnp.dot(left, query_w[k][...], preferred_element_type=F32)
            kv_term = jnp.dot(left, keyval_w[k][...], preferred_element_type=F32)
            query = q_term if query is None else query + q_term
            keyval = kv_term if keyval is None else keyval + kv_term
            k += 1
    if not last:
        query_out[...] = query
        keyval_out[...] = keyval
        return
    q_cos, q_sin, kv_cos, kv_sin = [t[...] for t in tables]
    for head in range(query.shape[1] // HD):
        span = slice(head * HD, (head + 1) * HD)
        part = query[:, span]
        query_out[:, span] = (part * q_cos + swap_members(part) * q_sin).astype(BF)
    turned = (keyval * kv_cos + swap_members(keyval) * kv_sin).astype(BF)
    to = lax.broadcasted_iota(jnp.int32, (HD, HD), 0)
    came = lax.broadcasted_iota(jnp.int32, (HD, HD), 1)
    order = jnp.where(came == to % 16 // 2 * 16 + to // 16 * 2 + to % 2, 1.0, 0.0).astype(BF)
    keyval_out[...] = lax.dot_general(
        order, turned, (((1,), (1,)), ((), ())), preferred_element_type=F32
    ).astype(BF)


def project(pieces, index, w_query, w_keyval, total, tables, block):
    pieces = [p if p.ndim == 3 else p[None] for p in pieces]
    counts = tuple(p.shape[0] for p in pieces)
    n = sum(counts)
    rows, width = pieces[0].shape[1:]
    columns = w_query.shape[1]
    last = tables is not None
    skip = block * (BLOCK // TILE)
    in_specs = [
        pl.BlockSpec((c, TILE, width), lambda i, p: (0, i, 0)) for c in counts
    ]
    for cols in (columns, HD):
        in_specs += [
            pl.BlockSpec((width, cols), lambda i, p, k=k: (p[k], 0)) for k in range(n)
        ]
    operands = pieces + [w_query] * n + [w_keyval] * n
    if total is not None:
        in_specs += [
            pl.BlockSpec((TILE, columns), lambda i, p: (i + skip, 0)),
            pl.BlockSpec((TILE, HD), lambda i, p: (i + skip, 0)),
        ]
        operands += list(total)
    if last:
        in_specs += [pl.BlockSpec((TILE, HD), lambda i, p: (i + skip, 0))] * 4
        operands += list(tables)
        out_shape = (
            jax.ShapeDtypeStruct((rows, columns), BF),
            jax.ShapeDtypeStruct((HD, rows), BF),
        )
        kv_spec = pl.BlockSpec((HD, TILE), lambda i, p: (0, i))
    else:
        out_shape = (
            jax.ShapeDtypeStruct((rows, columns), F32),
            jax.ShapeDtypeStruct((rows, HD), F32),
        )
        kv_spec = pl.BlockSpec((TILE, HD), lambda i, p: (i, 0))
    return pl.pallas_call(
        functools.partial(project_kernel, counts, total is not None, last),
        out_shape=out_shape,
        grid_spec=pltpu.PrefetchScalarGridSpec(
            num_scalar_prefetch=1,
            grid=(rows // TILE,),
            in_specs=in_specs,
            out_specs=[pl.BlockSpec((TILE, columns), lambda i, p: (i, 0)), kv_spec],
        ),
        compiler_params=params(48),
        cost_estimate=pl.CostEstimate(
            flops=2 * rows * n * width * (columns + HD),
            bytes_accessed=n * width * (rows + columns + HD) * 2,
            transcendentals=0,
        ),
        name="project",
    )(index, *operands)


def attend_kernel(block, plan_ref, query_ref, *refs):
    heads_ref = refs[-1]
    keyvals = refs[:-1]
    scale = 1.0 / math.sqrt(HD)
    local_heads = query_ref.shape[1] // HD
    for tile in range(BLOCK // TILE):
        here = block * (BLOCK // TILE) + tile
        rows = here * TILE + lax.broadcasted_iota(jnp.int32, (TILE, 1), 0)
        begin = jnp.zeros((TILE, 1), jnp.int32)
        for s in range(8):
            begin = jnp.where(rows >= plan_ref[0, s], plan_ref[0, s], begin)
        filled = rows < plan_ref[1, 7]
        seen = []
        for there in range(max(here - 1, 0), here + 1):
            columns = there * TILE + lax.broadcasted_iota(jnp.int32, (TILE, TILE), 1)
            allowed = (columns >= begin) & (columns <= rows)
            source = keyvals[-1] if there * TILE >= block * BLOCK else keyvals[0]
            first = there * TILE % BLOCK
            seen.append((allowed, source, slice(first, first + TILE)))
        for head in range(local_heads):
            span = slice(head * HD, (head + 1) * HD)
            query = query_ref[tile * TILE : (tile + 1) * TILE, span]
            scores = []
            for allowed, source, at in seen:
                raw = jnp.dot(query, source[0:HD, at], preferred_element_type=F32)
                scores.append(jnp.where(allowed, raw * scale, -1e30))
            top = functools.reduce(
                jnp.maximum, [jnp.max(s, axis=1, keepdims=True) for s in scores]
            )
            shifted = [jnp.exp(s - top) for s in scores]
            norm = sum(jnp.sum(s, axis=1, keepdims=True) for s in shifted)
            result = jnp.zeros((TILE, HD), F32)
            for part, (_, source, at) in zip(shifted, seen):
                weights = (part / norm).astype(BF)
                result += lax.dot_general(
                    weights,
                    source[HD : 2 * HD, at],
                    (((1,), (1,)), ((), ())),
                    preferred_element_type=F32,
                )
            heads_ref[tile * TILE : (tile + 1) * TILE, span] = jnp.where(
                filled, result, 0.0
            ).astype(BF)


def attend(block, plan, query, keyvals):
    return pl.pallas_call(
        functools.partial(attend_kernel, block),
        out_shape=jax.ShapeDtypeStruct(query.shape, BF),
        in_specs=[pl.BlockSpec(memory_space=pltpu.SMEM)]
        + [pl.BlockSpec(memory_space=pltpu.VMEM)] * (1 + len(keyvals)),
        out_specs=pl.BlockSpec(memory_space=pltpu.VMEM),
        compiler_params=params(32),
        cost_estimate=pl.CostEstimate(
            flops=4 * BLOCK * 2 * TILE * query.shape[1],
            bytes_accessed=2 << 20,
            transcendentals=BLOCK * 2 * TILE * 4,
        ),
        name="attend",
    )(plan, query, *keyvals)


def chunks_kernel(adds, *refs):
    refs = list(refs)
    refs.pop(0)
    heads = refs.pop(0)[...]
    n = len(adds)
    weights = [refs.pop(0) for _ in range(n)]
    out_ref = refs.pop()
    for k in range(n):
        total = jnp.dot(heads, weights[k][...], preferred_element_type=F32)
        for _ in range(adds[k]):
            total += refs.pop(0)[0].astype(F32)
        out_ref[k] = total.astype(BF)


def chunks(heads, w_out, index, adds):
    rows, depth = heads.shape
    width = 512
    n = len(adds)
    in_specs = [pl.BlockSpec((TILE, depth), lambda i, p: (i, 0))]
    in_specs += [
        pl.BlockSpec((depth, width), lambda i, p, k=k: (0, p[k])) for k in range(n)
    ]
    operands = [heads] + [w_out] * n
    for terms in adds:
        for array, place in terms:
            in_specs.append(
                pl.BlockSpec((1, TILE, width), lambda i, p, at=place: (at, i, 0))
            )
            operands.append(array)
    return pl.pallas_call(
        functools.partial(chunks_kernel, tuple(len(a) for a in adds)),
        out_shape=jax.ShapeDtypeStruct((n, rows, width), BF),
        grid_spec=pltpu.PrefetchScalarGridSpec(
            num_scalar_prefetch=1,
            grid=(rows // TILE,),
            in_specs=in_specs,
            out_specs=pl.BlockSpec((n, TILE, width), lambda i, p: (0, i, 0)),
        ),
        compiler_params=params(32),
        cost_estimate=pl.CostEstimate(
            flops=2 * rows * depth * width * n,
            bytes_accessed=2 * n * width * (rows + depth) * 2,
            transcendentals=0,
        ),
        name="chunks",
    )(index, *operands)


def gather_chips(value):
    own = jnp.stack([value, send(value, TO_CORE)])
    across = send(value, TO_X)
    up = send(own, TO_Y)
    across = jnp.stack([across, send(across, TO_CORE)])
    far = send(up[:1], TO_Y)
    down = send(up, TO_CORE)
    across_up = send(across, TO_Y)
    far_other = send(far, TO_CORE)
    across_far = send(across_up[:1], TO_Y)
    across_down = send(across_up, TO_CORE)
    across_far_other = send(across_far, TO_CORE)
    return [
        own, up, down, far, far_other,
        across, across_up, across_down, across_far, across_far_other,
    ]


def gather_order(x, y, c):
    way = 1 - 2 * c
    order = []
    for side in (x, 1 - x):
        for row, core in (
            (y, c), (y, 1 - c), (y - way, c), (y - way, 1 - c),
            (y + way, 1 - c), (y + way, c), (y + 2, c), (y + 2, 1 - c),
        ):
            order.append(side * 8 + (row + 4) % 4 * 2 + core)
    return jnp.stack(order).astype(jnp.int32)


def scatter_sum(heads, w_out, x, y, c):
    way = 1 - 2 * c

    def at(*places):
        return jnp.stack(
            [side * 8 + (row + 4) % 4 * 2 + core for side, row, core in places]
        ).astype(jnp.int32)

    sides = (1 - x, x)
    for_core = []
    for side in sides:
        index = at((side, y + 2, 1 - c), (side, y - way, 1 - c), (side, y - way, c))
        for_core.append(send(chunks(heads, w_out, index, [[], [], []]), TO_CORE))
    far = []
    for side, other in zip(sides, for_core):
        far.append(send(chunks(heads, w_out, at((side, y + 2, c)), [[(other, 0)]]), TO_Y))
    near = []
    for side, other, passed in zip(sides, for_core, far):
        index = at((side, y + way, c), (side, y + way, 1 - c))
        adds = [[(other, 1), (passed, 0)], [(other, 2)]]
        near.append(send(chunks(heads, w_out, index, adds), TO_Y))
    crossed = None
    for side, came in zip(sides, near):
        shared = send(chunks(heads, w_out, at((side, y, 1 - c)), [[(came, 1)]]), TO_CORE)
        adds = [(came, 0), (shared, 0)]
        if crossed is not None:
            adds.append((crossed, 0))
        result = chunks(heads, w_out, at((side, y, c)), [adds])
        if crossed is None:
            crossed = send(result, TO_X)
    return result[0]


def rotary_tables(position, member):
    lanes = jnp.arange(HD, dtype=jnp.int32)
    sign = jnp.where(lanes % 2 == 0, -1.0, 1.0).astype(F32)

    def table(pairs):
        frequency = jnp.exp(pairs.astype(F32) * (-2.0 * math.log(rope_base) / HD))
        angles = position.astype(F32)[:, None] * frequency[None, :]
        return jnp.cos(angles), jnp.sin(angles) * sign[None, :]

    q_cos, q_sin = table(lanes // 2)
    columns = member * HD + lanes
    kv_cos, kv_sin = table(columns // (2 * KVH) % (HD // 2))
    keys = member < KVH
    return q_cos, q_sin, jnp.where(keys, kv_cos, 1.0), jnp.where(keys, kv_sin, 0.0)


def body(rollout, lengths, target, w_query, w_keyval, w_out):
    member = lax.axis_index("tp")
    x, y, c = member // 8, member // 2 % 4, member % 2
    section_ids = jnp.arange(8, dtype=jnp.int32)
    own_lengths = lengths[0]
    chosen = target[0][None, :] == section_ids[:, None]
    before = jnp.cumsum(own_lengths) - own_lengths
    count_to = jnp.sum(jnp.where(chosen, own_lengths[None, :], 0), axis=1)
    start_to = jnp.sum(jnp.where(chosen, before[None, :], 0), axis=1)
    sent_from = jnp.minimum(start_to // ALIGN * ALIGN, rollout.shape[0] - SENT)
    facts = jnp.stack([count_to, start_to - sent_from], axis=1)
    facts = lax.all_to_all(facts, "sec", split_axis=0, concat_axis=0, tiled=True)
    outgoing = cut(rollout, sent_from)
    arrived = [
        lax.all_to_all(o, "sec", split_axis=0, concat_axis=0, tiled=True).reshape(
            8 * SENT, o.shape[2]
        )
        for o in outgoing
    ]
    counts, shifts = facts[:, 0], facts[:, 1]
    ends = jnp.cumsum(counts)
    offsets = ends - counts
    plan = jnp.stack([offsets, ends, section_ids * SENT + shifts - offsets])
    row_ids = jnp.arange(CAP, dtype=jnp.int32)
    begin = jnp.max(
        jnp.where(row_ids[:, None] >= offsets[None, :], offsets[None, :], 0), axis=1
    )
    tables = rotary_tables(row_ids - begin, member)

    order = gather_order(x, y, c)
    first = pack(arrived[0], plan)
    second = pack(arrived[1], plan)
    total = project(gather_chips(first), order * 2, w_query[0], w_keyval[0], None, None, 0)
    keyvals = []
    results = []
    for block in range(CAP // BLOCK):
        rows = second[block * BLOCK : (block + 1) * BLOCK]
        query, keyval = project(
            gather_chips(rows), order * 2 + 1, w_query[0], w_keyval[0], total, tables, block
        )
        spread = jnp.repeat(keyval.reshape(KVH, 2 * KVH, BLOCK), 2, axis=0)
        spread = lax.all_to_all(spread, "tp", split_axis=0, concat_axis=0, tiled=True)
        keyvals.append(spread.reshape(2 * HD, BLOCK))
        heads = attend(block, plan, query, keyvals[-2:])
        results.append(scatter_sum(heads, w_out[0], x, y, c))
    return jnp.concatenate(results, axis=0)


def solution(mesh):
    placed = (
        P("sec", "tp"),
        P("sec", None),
        P("sec", None),
        P("sec", None, "tp"),
        P("sec", None, "tp"),
        P("sec", "tp", None),
    )
    return jax.shard_map(
        body, mesh=mesh, in_specs=placed, out_specs=P("sec", "tp"), check_vma=False
    )
```

```python
import functools
import math

import jax
import jax.numpy as jnp
from jax import lax
from jax.experimental import pallas as pl
from jax.experimental.pallas import tpu as pltpu
from jax.sharding import PartitionSpec as P

HQ = 64
KVH = 8
HD = 128
CAP = 1024
SLOT = 256
ALIGN = 16
SENT = SLOT + ALIGN
TILE = 256
BLOCK = 512
rope_base = 500000.0
BF = jnp.bfloat16
F32 = jnp.float32


def params():
    return pltpu.CompilerParams(vmem_limit_bytes=14 << 20)


def permutation(move):
    pairs = []
    for t in range(16):
        x, y, c = move(t // 8, t // 2 % 4, t % 2)
        pairs.append((t, x % 2 * 8 + y % 4 * 2 + c % 2))
    return pairs


TO_CORE = permutation(lambda x, y, c: (x, y, c + 1))
TO_X = permutation(lambda x, y, c: (x + 1, y, c))
TO_Y = permutation(lambda x, y, c: (x, y + 1 - 2 * c, c))


def after(value, *others):
    return lax.optimization_barrier((value, *others))[0]


class Line:
    def __init__(self):
        self.last = None

    def next(self, value):
        return value if self.last is None else after(value, self.last)

    def add(self, result):
        self.last = jax.tree.leaves(result)[0]
        return result


def send(value, pairs):
    return lax.ppermute(value, "tp", pairs)


def in_hbm(array):
    return pltpu.with_memory_space_constraint(array, pltpu.HBM)


def cut_kernel(start_ref, rollout_ref, sent_ref):
    for d in range(8):
        row = pl.multiple_of(start_ref[d], ALIGN)
        sent_ref[d] = rollout_ref[pl.ds(row, SENT), :]


def cut(rollout, starts):
    return pl.pallas_call(
        cut_kernel,
        out_shape=jax.ShapeDtypeStruct((8, SENT, rollout.shape[1]), BF),
        in_specs=[
            pl.BlockSpec(memory_space=pltpu.SMEM),
            pl.BlockSpec(memory_space=pltpu.VMEM),
        ],
        out_specs=pl.BlockSpec(memory_space=pltpu.VMEM),
        compiler_params=params(),
        name="cut",
    )(starts, rollout)


def pack_kernel(plan_ref, arrived_ref, packed_ref, total_ref):
    first = pl.program_id(0) * TILE
    rows = first + lax.broadcasted_iota(jnp.int32, (TILE, 1), 0)
    slots = lax.broadcasted_iota(jnp.int32, (TILE, SENT), 1)
    total_ref[...] = jnp.zeros_like(total_ref)
    for s in range(8):
        begin, end = plan_ref[0, s], plan_ref[1, s]

        @pl.when((begin < first + TILE) & (end > first))
        def _():
            source = jnp.where(
                (rows >= begin) & (rows < end), rows + plan_ref[2, s], -1
            )
            picked = jnp.where(slots == source, 1.0, 0.0).astype(BF)
            total_ref[...] += jnp.dot(
                picked, arrived_ref[s], preferred_element_type=F32
            )

    packed_ref[...] = total_ref[...].astype(BF)


def pack(arrived, plan):
    width = arrived.shape[2]
    return pl.pallas_call(
        pack_kernel,
        out_shape=jax.ShapeDtypeStruct((CAP, width), BF),
        grid_spec=pltpu.PrefetchScalarGridSpec(
            num_scalar_prefetch=1,
            grid=(CAP // TILE,),
            in_specs=[pl.BlockSpec(memory_space=pltpu.VMEM)],
            out_specs=pl.BlockSpec((TILE, width), lambda i, p: (i, 0)),
            scratch_shapes=[pltpu.VMEM((TILE, width), F32)],
        ),
        compiler_params=params(),
        name="pack",
    )(plan, arrived)


def swap_members(values):
    lanes = lax.broadcasted_iota(jnp.int32, values.shape, 1)
    return jnp.where(
        lanes % 2 == 0, pltpu.roll(values, HD - 1, 1), pltpu.roll(values, 1, 1)
    )


def project_kernel(counts, has_total, last, index_ref, *refs):
    refs = list(refs)
    pieces = [refs.pop(0) for _ in counts]
    query_w, keyval_w = refs.pop(0), refs.pop(0)
    total_ref = refs.pop(0) if has_total else None
    tables = [refs.pop(0) for _ in range(4)] if last else None
    weights_ref, sems = refs[-2:]
    refs = refs[:-2]
    columns = query_w.shape[1]
    depth = pieces[0].shape[2]
    copies = []
    for k in range(sum(counts)):
        rows = pl.ds(pl.multiple_of(index_ref[k] * depth, depth), depth)
        copies.append((
            pltpu.make_async_copy(
                query_w.at[rows, :], weights_ref.at[k, :, pl.ds(0, columns)], sems.at[k, 0]
            ),
            pltpu.make_async_copy(
                keyval_w.at[rows, :], weights_ref.at[k, :, pl.ds(columns, HD)], sems.at[k, 1]
            ),
        ))

    @pl.when(pl.program_id(0) == 0)
    def _():
        for pair in copies:
            for copy in pair:
                copy.start()

    query = total_ref[:, :columns] if has_total else 0.0
    keyval = total_ref[:, columns:] if has_total else 0.0
    k = 0
    for ref, count in zip(pieces, counts):
        for j in range(count):

            @pl.when(pl.program_id(0) == 0)
            def _(k=k):
                for copy in copies[k]:
                    copy.wait()

            left = ref[j]
            query += jnp.dot(left, weights_ref[k, :, :columns], preferred_element_type=F32)
            keyval += jnp.dot(left, weights_ref[k, :, columns:], preferred_element_type=F32)
            k += 1
    if not last:
        refs[0][:, :columns] = query
        refs[0][:, columns:] = keyval
        return
    query_out, keyval_out = refs
    q_cos, q_sin, kv_cos, kv_sin = [t[...] for t in tables]
    for head in range(columns // HD):
        span = slice(head * HD, (head + 1) * HD)
        part = query[:, span]
        query_out[:, span] = (part * q_cos + swap_members(part) * q_sin).astype(BF)
    turned = (keyval * kv_cos + swap_members(keyval) * kv_sin).astype(BF)
    to = lax.broadcasted_iota(jnp.int32, (HD, HD), 0)
    came = lax.broadcasted_iota(jnp.int32, (HD, HD), 1)
    order = jnp.where(came == to % 16 // 2 * 16 + to // 16 * 2 + to % 2, 1.0, 0.0).astype(BF)
    turned = lax.dot_general(
        order, turned, (((1,), (1,)), ((), ())), preferred_element_type=F32
    ).astype(BF)
    for member in range(2 * KVH):
        keyval_out[member] = turned[member // 2 * 16 : member // 2 * 16 + 16]


def project(pieces, index, w_query, w_keyval, rows, total=None, tables=None, block=0):
    counts = tuple(p.shape[0] for p in pieces)
    n = sum(counts)
    width = pieces[0].shape[2]
    columns = w_query.shape[1]
    last = tables is not None

    def skip(array, axis):
        return block * (BLOCK // TILE) if array.shape[axis] > rows else 0

    in_specs = [
        pl.BlockSpec((p.shape[0], TILE, width), lambda i, _, at=skip(p, 1): (0, i + at, 0))
        for p in pieces
    ]
    in_specs += [pl.BlockSpec(memory_space=pltpu.HBM)] * 2
    operands = list(pieces) + [in_hbm(w_query), in_hbm(w_keyval)]
    if total is not None:
        at = skip(total, 0)
        in_specs.append(pl.BlockSpec((TILE, columns + HD), lambda i, _: (i + at, 0)))
        operands.append(in_hbm(total))
    if last:
        first = skip(tables[0], 0)
        in_specs += [pl.BlockSpec((TILE, HD), lambda i, _: (i + first, 0))] * 4
        operands += [in_hbm(t) for t in tables]
        out_shape = (
            jax.ShapeDtypeStruct((rows, columns), BF),
            jax.ShapeDtypeStruct((2 * KVH, 16, rows), BF),
        )
        out_specs = [
            pl.BlockSpec((TILE, columns), lambda i, _: (i, 0)),
            pl.BlockSpec((2 * KVH, 16, TILE), lambda i, _: (0, 0, i)),
        ]
    else:
        out_shape = jax.ShapeDtypeStruct((rows, columns + HD), F32)
        out_specs = pl.BlockSpec((TILE, columns + HD), lambda i, _: (i, 0))
    return pl.pallas_call(
        functools.partial(project_kernel, counts, total is not None, last),
        out_shape=out_shape,
        grid_spec=pltpu.PrefetchScalarGridSpec(
            num_scalar_prefetch=1,
            grid=(rows // TILE,),
            in_specs=in_specs,
            out_specs=out_specs,
            scratch_shapes=[
                pltpu.VMEM((n, width, columns + HD), BF),
                pltpu.SemaphoreType.DMA((n, 2)),
            ],
        ),
        compiler_params=params(),
        name="project",
    )(index, *operands)


def attend_kernel(block, plan_ref, query_ref, *refs):
    keyval_refs, heads_ref = refs[:-1], refs[-1]
    scale = 1.0 / math.sqrt(HD)
    local_heads = query_ref.shape[1] // HD

    def columns_of(there, member):
        part, first = there * TILE // BLOCK, there * TILE % BLOCK
        return keyval_refs[part][member * HD : (member + 1) * HD, first : first + TILE]

    for tile in range(BLOCK // TILE):
        here = block * (BLOCK // TILE) + tile
        rows = here * TILE + lax.broadcasted_iota(jnp.int32, (TILE, 1), 0)
        begin = jnp.zeros((TILE, 1), jnp.int32)
        for s in range(8):
            begin = jnp.where(rows >= plan_ref[0, s], plan_ref[0, s], begin)
        filled = rows < plan_ref[1, 7]
        seen = []
        for there in range(max(here - 1, 0), here + 1):
            columns = there * TILE + lax.broadcasted_iota(jnp.int32, (TILE, TILE), 1)
            allowed = (columns >= begin) & (columns <= rows)
            seen.append((allowed, columns_of(there, 0), columns_of(there, 1)))
        for head in range(local_heads):
            span = slice(head * HD, (head + 1) * HD)
            query = query_ref[tile * TILE : (tile + 1) * TILE, span]
            scores = []
            for allowed, key, _ in seen:
                raw = jnp.dot(query, key, preferred_element_type=F32)
                scores.append(jnp.where(allowed, raw * scale, -1e30))
            top = functools.reduce(
                jnp.maximum, [jnp.max(s, axis=1, keepdims=True) for s in scores]
            )
            shifted = [jnp.exp(s - top) for s in scores]
            norm = sum(jnp.sum(s, axis=1, keepdims=True) for s in shifted)
            result = jnp.zeros((TILE, HD), F32)
            for part, (_, _, value) in zip(shifted, seen):
                weights = (part / norm).astype(BF)
                result += lax.dot_general(
                    weights, value, (((1,), (1,)), ((), ())), preferred_element_type=F32
                )
            heads_ref[tile * TILE : (tile + 1) * TILE, span] = jnp.where(
                filled, result, 0.0
            ).astype(BF)


def attend(block, plan, query, keyvals):
    return pl.pallas_call(
        functools.partial(attend_kernel, block),
        out_shape=jax.ShapeDtypeStruct(query.shape, BF),
        in_specs=[
            pl.BlockSpec(memory_space=pltpu.SMEM),
            pl.BlockSpec(memory_space=pltpu.VMEM),
        ]
        + [pl.BlockSpec(memory_space=pltpu.VMEM)] * len(keyvals),
        out_specs=pl.BlockSpec(memory_space=pltpu.VMEM),
        compiler_params=params(),
        name="attend",
    )(plan, query, *keyvals)


def chunks_kernel(groups, adds, index_ref, heads_ref, w_out, *refs):
    n = len(adds)
    refs = list(refs)
    weights_ref, sems = refs[-2:]
    outs = refs[-2 - len(groups) : -2]
    width = weights_ref.shape[2]
    copies = []
    for k in range(n):
        columns = pl.ds(pl.multiple_of(index_ref[k] * width, width), width)
        copies.append(
            pltpu.make_async_copy(w_out.at[:, columns], weights_ref.at[k], sems.at[k])
        )

    @pl.when(pl.program_id(0) == 0)
    def _():
        for copy in copies:
            copy.start()

    k = 0
    for out, size in zip(outs, groups):
        for j in range(size):

            @pl.when(pl.program_id(0) == 0)
            def _(k=k):
                copies[k].wait()

            total = jnp.dot(heads_ref[...], weights_ref[k], preferred_element_type=F32)
            for _ in range(adds[k]):
                total += refs.pop(0)[0].astype(F32)
            out[j] = total.astype(BF)
            k += 1


def chunks(heads, w_out, index, groups, adds):
    rows, depth = heads.shape
    width = 512
    n = len(adds)
    in_specs = [
        pl.BlockSpec((TILE, depth), lambda i, p: (i, 0)),
        pl.BlockSpec(memory_space=pltpu.HBM),
    ]
    operands = [heads, in_hbm(w_out)]
    for terms in adds:
        for array, place in terms:
            in_specs.append(
                pl.BlockSpec((1, TILE, width), lambda i, p, at=place: (at, i, 0))
            )
            operands.append(array)
    return pl.pallas_call(
        functools.partial(chunks_kernel, groups, tuple(len(a) for a in adds)),
        out_shape=[jax.ShapeDtypeStruct((g, rows, width), BF) for g in groups],
        grid_spec=pltpu.PrefetchScalarGridSpec(
            num_scalar_prefetch=1,
            grid=(rows // TILE,),
            in_specs=in_specs,
            out_specs=[pl.BlockSpec((g, TILE, width), lambda i, p: (0, i, 0)) for g in groups],
            scratch_shapes=[
                pltpu.VMEM((n, depth, width), BF),
                pltpu.SemaphoreType.DMA((n,)),
            ],
        ),
        compiler_params=params(),
        name="chunks",
    )(index, *operands)


def gather_order(x, y, c):
    way = 1 - 2 * c
    places = [(x, y, c), (x, y, 1 - c), (x, y - way, c), (x, y - way, 1 - c)]
    places += [(x, y + way, 1 - c), (x, y + way, c)]
    places += [(1 - x, y, c), (1 - x, y, 1 - c), (x, y + 2, c), (x, y + 2, 1 - c)]
    places += [(1 - x, y - way, c), (1 - x, y - way, 1 - c)]
    places += [(1 - x, y + way, 1 - c), (1 - x, y + way, c)]
    places += [(1 - x, y + 2, c), (1 - x, y + 2, 1 - c)]
    return jnp.stack(
        [side * 8 + (row + 4) % 4 * 2 + core for side, row, core in places]
    ).astype(jnp.int32)


def rotary_tables(position, member):
    lanes = jnp.arange(HD, dtype=jnp.int32)
    sign = jnp.where(lanes % 2 == 0, -1.0, 1.0).astype(F32)

    def table(pairs):
        frequency = jnp.exp(pairs.astype(F32) * (-2.0 * math.log(rope_base) / HD))
        angles = position.astype(F32)[:, None] * frequency[None, :]
        return jnp.cos(angles), jnp.sin(angles) * sign[None, :]

    q_cos, q_sin = table(lanes // 2)
    columns = member * HD + lanes
    kv_cos, kv_sin = table(columns // (2 * KVH) % (HD // 2))
    keys = member < KVH
    return q_cos, q_sin, jnp.where(keys, kv_cos, 1.0), jnp.where(keys, kv_sin, 0.0)


def body(rollout, lengths, target, w_query, w_keyval, w_out):
    member = lax.axis_index("tp")
    x, y, c = member // 8, member // 2 % 4, member % 2
    section_ids = jnp.arange(8, dtype=jnp.int32)
    own_lengths = lengths[0]
    chosen = target[0][None, :] == section_ids[:, None]
    before = jnp.cumsum(own_lengths) - own_lengths
    start_to = jnp.sum(jnp.where(chosen, before[None, :], 0), axis=1)
    sent_from = jnp.minimum(start_to // ALIGN * ALIGN, rollout.shape[0] - SENT)
    count_to = jnp.sum(jnp.where(chosen, own_lengths[None, :], 0), axis=1)
    facts = jnp.stack([count_to, start_to - sent_from], axis=1)
    outgoing = cut(rollout, sent_from)
    arrived = lax.all_to_all(outgoing, "sec", split_axis=0, concat_axis=0, tiled=True)
    facts = lax.all_to_all(facts, "sec", split_axis=0, concat_axis=0, tiled=True)
    counts, shifts = facts[:, 0], facts[:, 1]
    ends = jnp.cumsum(counts)
    offsets = ends - counts
    plan = jnp.stack([offsets, ends, shifts - offsets])
    row_ids = jnp.arange(CAP, dtype=jnp.int32)
    begin = jnp.max(
        jnp.where(row_ids[:, None] >= offsets[None, :], offsets[None, :], 0), axis=1
    )
    order = gather_order(x, y, c)
    weights = w_query[0], w_keyval[0]
    w_out = w_out[0]
    line = Line()
    way = 1 - 2 * c
    sides = (1 - x, x)

    def at(*places):
        return jnp.stack(
            [side * 8 + (row + 4) % 4 * 2 + core for side, row, core in places]
        ).astype(jnp.int32)

    def move(value, pairs):
        return send(line.next(value), pairs)

    def stack(*arrays):
        return line.add(jnp.stack([line.next(arrays[0]), *arrays[1:]]))

    def part(value, *index):
        return line.add(line.next(value)[index])

    def projected(pieces, index, *more):
        return line.add(project(pieces, line.next(index), *weights, *more))

    def spread(keyval):
        keyval = lax.all_to_all(
            line.next(keyval), "tp", split_axis=0, concat_axis=0, tiled=True
        )
        return keyval.reshape(2 * HD, BLOCK)

    def attended(block, query, keyvals):
        return line.add(attend(block, line.next(plan), query, keyvals))

    def join(*arrays):
        *arrays, line.last = lax.optimization_barrier((*arrays, line.last))
        return arrays

    def summed(heads, places, groups, adds):
        index = line.next(at(*places))
        return line.add(chunks(heads, w_out, index, groups, adds))

    def for_core(heads, places):
        parts = summed(heads, places, (1,) * len(places), [[]] * len(places))
        return [send(p, TO_CORE) for p in parts]

    def far_for_core(heads):
        return for_core(heads, [(side, y + 2, 1 - c) for side in sides])

    def near_for_core(heads):
        places = []
        for side in sides:
            places += [(side, y - way, 1 - c), (side, y - way, c)]
        return for_core(heads, places)

    def far_sums(heads, passed):
        places = [(side, y + 2, c) for side in sides]
        adds = [[(p, 0)] for p in passed]
        return send(summed(heads, places, (2,), adds)[0], TO_Y)

    def near_sums(heads, passed, far, groups):
        places, adds = [], []
        for i, side in enumerate(sides):
            places += [(side, y + way, c), (side, y + way, 1 - c)]
            adds += [[(passed[2 * i], 0), (far, i)], [(passed[2 * i + 1], 0)]]
        return summed(heads, places, groups, adds)

    def last_sum(i, heads, near, place, *more):
        shared = summed(heads, [(sides[i], y, 1 - c)], (1,), [[(near, place + 1)]])[0]
        terms = [(near, place), (send(shared, TO_CORE), 0)] + [(t, 0) for t in more]
        return summed(heads, [(sides[i], y, c)], (1,), [terms])[0]


    value = line.add(pack(arrived, plan))
    across = send(value, TO_X)
    up = send(value, TO_Y)
    other = send(value, TO_CORE)
    up_other = send(other, TO_Y)
    position = line.next(row_ids) - begin
    tables = line.add(rotary_tables(position, member))
    total = projected([value[None], other[None]], order[:2], CAP)
    across, up, up_other = join(across, up, up_other)
    far = send(up, TO_Y)
    there_up1 = send(jnp.stack([up[BLOCK:], up_other[BLOCK:]]), TO_X)
    across_other = send(across, TO_CORE)
    there_up0 = send(jnp.stack([across[:BLOCK], across_other[:BLOCK]]), TO_Y)
    down, down_other = send(up, TO_CORE), send(up_other, TO_CORE)
    pieces = [up, up_other, down, down_other, across, across_other]
    total = projected([p[None] for p in pieces], order[2:8], CAP, total)
    far, *there_up = join(far, there_up0, there_up1)
    there_far = [send(there_up[0][:1], TO_Y), send(far[None, BLOCK:], TO_X)]
    there_down = [send(u, TO_CORE) for u in there_up]
    far_other = send(far, TO_CORE)
    pieces = [far[None], far_other[None], there_up[0], there_down[0]]
    total0 = projected(pieces, order[8:14], BLOCK, total, None, 0)
    there_far0, far = join(there_far[0], far)
    pieces = [there_far0, send(there_far0, TO_CORE)]
    query0, keyval0 = projected(pieces, order[14:], BLOCK, total0, tables, 0)
    keyval0 = spread(keyval0)
    pieces = [far[None], far_other[None], there_up[1], there_down[1]]
    there_far_other1 = send(there_far[1], TO_CORE)
    index = after(order[8:14], there_far_other1)
    total1 = projected(pieces, index, BLOCK, total, None, 1)
    heads0 = attended(0, query0, [keyval0])
    far0 = far_sums(heads0, far_for_core(heads0))
    passed = near_for_core(heads0)
    pieces = [there_far[1], there_far_other1]
    query1, keyval1 = projected(pieces, order[14:], BLOCK, total1, tables, 1)
    keyval1 = spread(keyval1)
    near0 = near_sums(heads0, passed, far0, (4,))[0]
    near0 = send(after(near0, keyval1), TO_Y)
    heads1 = attended(1, query1, [keyval0, keyval1])
    far1 = far_sums(heads1, far_for_core(heads1))
    passed = near_for_core(heads1)
    crossed0 = send(last_sum(0, after(heads0, *passed), near0, 0), TO_X)
    near1 = [send(t, TO_Y) for t in near_sums(heads1, passed, far1, (2, 2))]
    result0 = last_sum(1, heads0, near0, 2, crossed0)
    crossed1 = send(last_sum(0, heads1, near1[0], 0), TO_X)
    result1 = last_sum(1, heads1, near1[1], 0, crossed1)
    return jnp.concatenate([result0[0], result1[0]], axis=0)


def solution(mesh):
    placed = (
        P("sec", "tp"),
        P("sec", None),
        P("sec", None),
        P("sec", None, "tp"),
        P("sec", None, "tp"),
        P("sec", "tp", None),
    )
    return jax.shard_map(
        body, mesh=mesh, in_specs=placed, out_specs=P("sec", "tp"), check_vma=False
    )
```

```python
import functools
import math

import jax
import jax.numpy as jnp
from jax import lax
from jax.experimental import pallas as pl
from jax.experimental.pallas import tpu as pltpu
from jax.sharding import PartitionSpec as P

HQ = 64
KVH = 8
HD = 128
CAP = 1024
SLOT = 256
ALIGN = 16
SENT = SLOT + ALIGN
TILE = 256
BLOCK = 512
rope_base = 500000.0
BF = jnp.bfloat16
F32 = jnp.float32


def params():
    return pltpu.CompilerParams(vmem_limit_bytes=14 << 20)


def permutation(move):
    pairs = []
    for t in range(16):
        x, y, c = move(t // 8, t // 2 % 4, t % 2)
        pairs.append((t, x % 2 * 8 + y % 4 * 2 + c % 2))
    return pairs


TO_CORE = permutation(lambda x, y, c: (x, y, c + 1))
TO_X = permutation(lambda x, y, c: (x + 1, y, c))
TO_Y = permutation(lambda x, y, c: (x, y + 1 - 2 * c, c))


def after(value, *others):
    return lax.optimization_barrier((value, *others))[0]


class Line:
    def __init__(self):
        self.last = None

    def next(self, value):
        return value if self.last is None else after(value, self.last)

    def add(self, result):
        self.last = jax.tree.leaves(result)[0]
        return result


def send(value, pairs):
    return lax.ppermute(value, "tp", pairs)


def in_hbm(array):
    return pltpu.with_memory_space_constraint(array, pltpu.HBM)


def cut_kernel(start_ref, rollout_ref, sent_ref):
    for d in range(8):
        row = pl.multiple_of(start_ref[d], ALIGN)
        sent_ref[d] = rollout_ref[pl.ds(row, SENT), :]


def cut(rollout, starts):
    return pl.pallas_call(
        cut_kernel,
        out_shape=jax.ShapeDtypeStruct((8, SENT, rollout.shape[1]), BF),
        in_specs=[
            pl.BlockSpec(memory_space=pltpu.SMEM),
            pl.BlockSpec(memory_space=pltpu.VMEM),
        ],
        out_specs=pl.BlockSpec(memory_space=pltpu.VMEM),
        compiler_params=params(),
        name="cut",
    )(starts, rollout)


def pack_kernel(plan_ref, arrived_ref, packed_ref, total_ref):
    first = pl.program_id(0) * TILE
    rows = first + lax.broadcasted_iota(jnp.int32, (TILE, 1), 0)
    slots = lax.broadcasted_iota(jnp.int32, (TILE, SENT), 1)
    total_ref[...] = jnp.zeros_like(total_ref)
    for s in range(8):
        begin, end = plan_ref[0, s], plan_ref[1, s]

        @pl.when((begin < first + TILE) & (end > first))
        def _():
            source = jnp.where(
                (rows >= begin) & (rows < end), rows + plan_ref[2, s], -1
            )
            picked = jnp.where(slots == source, 1.0, 0.0).astype(BF)
            total_ref[...] += jnp.dot(
                picked, arrived_ref[s], preferred_element_type=F32
            )

    packed_ref[...] = total_ref[...].astype(BF)


def pack(arrived, plan):
    width = arrived.shape[2]
    return pl.pallas_call(
        pack_kernel,
        out_shape=jax.ShapeDtypeStruct((CAP, width), BF),
        grid_spec=pltpu.PrefetchScalarGridSpec(
            num_scalar_prefetch=1,
            grid=(CAP // TILE,),
            in_specs=[pl.BlockSpec(memory_space=pltpu.VMEM)],
            out_specs=pl.BlockSpec((TILE, width), lambda i, p: (i, 0)),
            scratch_shapes=[pltpu.VMEM((TILE, width), F32)],
        ),
        compiler_params=params(),
        name="pack",
    )(plan, arrived)


def swap_members(values):
    lanes = lax.broadcasted_iota(jnp.int32, values.shape, 1)
    return jnp.where(
        lanes % 2 == 0, pltpu.roll(values, HD - 1, 1), pltpu.roll(values, 1, 1)
    )


def project_kernel(counts, has_total, last, index_ref, *refs):
    refs = list(refs)
    pieces = [refs.pop(0) for _ in counts]
    query_w, keyval_w = refs.pop(0), refs.pop(0)
    total_ref = refs.pop(0) if has_total else None
    tables = [refs.pop(0) for _ in range(4)] if last else None
    weights_ref, sems = refs[-2:]
    refs = refs[:-2]
    columns = query_w.shape[1]
    depth = pieces[0].shape[2]
    copies = []
    for k in range(sum(counts)):
        rows = pl.ds(pl.multiple_of(index_ref[k] * depth, depth), depth)
        copies.append((
            pltpu.make_async_copy(
                query_w.at[rows, :], weights_ref.at[k, :, pl.ds(0, columns)], sems.at[k, 0]
            ),
            pltpu.make_async_copy(
                keyval_w.at[rows, :], weights_ref.at[k, :, pl.ds(columns, HD)], sems.at[k, 1]
            ),
        ))

    @pl.when(pl.program_id(0) == 0)
    def _():
        for pair in copies:
            for copy in pair:
                copy.start()

    query = total_ref[:, :columns] if has_total else 0.0
    keyval = total_ref[:, columns:] if has_total else 0.0
    k = 0
    for ref, count in zip(pieces, counts):
        for j in range(count):

            @pl.when(pl.program_id(0) == 0)
            def _(k=k):
                for copy in copies[k]:
                    copy.wait()

            left = ref[j]
            query += jnp.dot(left, weights_ref[k, :, :columns], preferred_element_type=F32)
            keyval += jnp.dot(left, weights_ref[k, :, columns:], preferred_element_type=F32)
            k += 1
    if not last:
        refs[0][:, :columns] = query
        refs[0][:, columns:] = keyval
        return
    query_out, keyval_out = refs
    q_cos, q_sin, kv_cos, kv_sin = [t[...] for t in tables]
    for head in range(columns // HD):
        span = slice(head * HD, (head + 1) * HD)
        part = query[:, span]
        query_out[:, span] = (part * q_cos + swap_members(part) * q_sin).astype(BF)
    turned = (keyval * kv_cos + swap_members(keyval) * kv_sin).astype(BF)
    to = lax.broadcasted_iota(jnp.int32, (HD, HD), 0)
    came = lax.broadcasted_iota(jnp.int32, (HD, HD), 1)
    order = jnp.where(came == to % 16 // 2 * 16 + to // 16 * 2 + to % 2, 1.0, 0.0).astype(BF)
    turned = lax.dot_general(
        order, turned, (((1,), (1,)), ((), ())), preferred_element_type=F32
    ).astype(BF)
    for member in range(2 * KVH):
        keyval_out[member] = turned[member // 2 * 16 : member // 2 * 16 + 16]


def project(pieces, index, w_query, w_keyval, rows, total=None, tables=None, block=0):
    counts = tuple(p.shape[0] for p in pieces)
    n = sum(counts)
    width = pieces[0].shape[2]
    columns = w_query.shape[1]
    last = tables is not None

    def skip(array, axis):
        return block * (BLOCK // TILE) if array.shape[axis] > rows else 0

    in_specs = [
        pl.BlockSpec((p.shape[0], TILE, width), lambda i, _, at=skip(p, 1): (0, i + at, 0))
        for p in pieces
    ]
    in_specs += [pl.BlockSpec(memory_space=pltpu.HBM)] * 2
    operands = list(pieces) + [in_hbm(w_query), in_hbm(w_keyval)]
    if total is not None:
        at = skip(total, 0)
        in_specs.append(pl.BlockSpec((TILE, columns + HD), lambda i, _: (i + at, 0)))
        operands.append(in_hbm(total))
    if last:
        first = skip(tables[0], 0)
        in_specs += [pl.BlockSpec((TILE, HD), lambda i, _: (i + first, 0))] * 4
        operands += [in_hbm(t) for t in tables]
        out_shape = (
            jax.ShapeDtypeStruct((rows, columns), BF),
            jax.ShapeDtypeStruct((2 * KVH, 16, rows), BF),
        )
        out_specs = [
            pl.BlockSpec((TILE, columns), lambda i, _: (i, 0)),
            pl.BlockSpec((2 * KVH, 16, TILE), lambda i, _: (0, 0, i)),
        ]
    else:
        out_shape = jax.ShapeDtypeStruct((rows, columns + HD), F32)
        out_specs = pl.BlockSpec((TILE, columns + HD), lambda i, _: (i, 0))
    return pl.pallas_call(
        functools.partial(project_kernel, counts, total is not None, last),
        out_shape=out_shape,
        grid_spec=pltpu.PrefetchScalarGridSpec(
            num_scalar_prefetch=1,
            grid=(rows // TILE,),
            in_specs=in_specs,
            out_specs=out_specs,
            scratch_shapes=[
                pltpu.VMEM((n, width, columns + HD), BF),
                pltpu.SemaphoreType.DMA((n, 2)),
            ],
        ),
        compiler_params=params(),
        name="project",
    )(index, *operands)


def attend_kernel(block, plan_ref, query_ref, *refs):
    keyval_refs, heads_ref = refs[:-1], refs[-1]
    scale = 1.0 / math.sqrt(HD)
    local_heads = query_ref.shape[1] // HD

    def columns_of(there, member):
        part, first = there * TILE // BLOCK, there * TILE % BLOCK
        return keyval_refs[part][member * HD : (member + 1) * HD, first : first + TILE]

    for tile in range(BLOCK // TILE):
        here = block * (BLOCK // TILE) + tile
        rows = here * TILE + lax.broadcasted_iota(jnp.int32, (TILE, 1), 0)
        begin = jnp.zeros((TILE, 1), jnp.int32)
        for s in range(8):
            begin = jnp.where(rows >= plan_ref[0, s], plan_ref[0, s], begin)
        filled = rows < plan_ref[1, 7]
        seen = []
        for there in range(max(here - 1, 0), here + 1):
            columns = there * TILE + lax.broadcasted_iota(jnp.int32, (TILE, TILE), 1)
            allowed = (columns >= begin) & (columns <= rows)
            seen.append((allowed, columns_of(there, 0), columns_of(there, 1)))
        for head in range(local_heads):
            span = slice(head * HD, (head + 1) * HD)
            query = query_ref[tile * TILE : (tile + 1) * TILE, span]
            scores = []
            for allowed, key, _ in seen:
                raw = jnp.dot(query, key, preferred_element_type=F32)
                scores.append(jnp.where(allowed, raw * scale, -1e30))
            top = functools.reduce(
                jnp.maximum, [jnp.max(s, axis=1, keepdims=True) for s in scores]
            )
            shifted = [jnp.exp(s - top) for s in scores]
            norm = sum(jnp.sum(s, axis=1, keepdims=True) for s in shifted)
            result = jnp.zeros((TILE, HD), F32)
            for part, (_, _, value) in zip(shifted, seen):
                weights = (part / norm).astype(BF)
                result += lax.dot_general(
                    weights, value, (((1,), (1,)), ((), ())), preferred_element_type=F32
                )
            heads_ref[tile * TILE : (tile + 1) * TILE, span] = jnp.where(
                filled, result, 0.0
            ).astype(BF)


def attend(block, plan, query, keyvals):
    return pl.pallas_call(
        functools.partial(attend_kernel, block),
        out_shape=jax.ShapeDtypeStruct(query.shape, BF),
        in_specs=[
            pl.BlockSpec(memory_space=pltpu.SMEM),
            pl.BlockSpec(memory_space=pltpu.VMEM),
        ]
        + [pl.BlockSpec(memory_space=pltpu.VMEM)] * len(keyvals),
        out_specs=pl.BlockSpec(memory_space=pltpu.VMEM),
        compiler_params=params(),
        name="attend",
    )(plan, query, *keyvals)


def chunks_kernel(groups, adds, index_ref, heads_ref, w_out, *refs):
    n = len(adds)
    refs = list(refs)
    weights_ref, sems = refs[-2:]
    outs = refs[-2 - len(groups) : -2]
    width = weights_ref.shape[2]
    copies = []
    for k in range(n):
        columns = pl.ds(pl.multiple_of(index_ref[k] * width, width), width)
        copies.append(
            pltpu.make_async_copy(w_out.at[:, columns], weights_ref.at[k], sems.at[k])
        )

    @pl.when(pl.program_id(0) == 0)
    def _():
        for copy in copies:
            copy.start()

    k = 0
    for out, size in zip(outs, groups):
        for j in range(size):

            @pl.when(pl.program_id(0) == 0)
            def _(k=k):
                copies[k].wait()

            total = jnp.dot(heads_ref[...], weights_ref[k], preferred_element_type=F32)
            for _ in range(adds[k]):
                total += refs.pop(0)[0].astype(F32)
            out[j] = total.astype(BF)
            k += 1


def chunks(heads, w_out, index, groups, adds):
    rows, depth = heads.shape
    width = 512
    n = len(adds)
    in_specs = [
        pl.BlockSpec((TILE, depth), lambda i, p: (i, 0)),
        pl.BlockSpec(memory_space=pltpu.HBM),
    ]
    operands = [heads, in_hbm(w_out)]
    for terms in adds:
        for array, place in terms:
            in_specs.append(
                pl.BlockSpec((1, TILE, width), lambda i, p, at=place: (at, i, 0))
            )
            operands.append(array)
    return pl.pallas_call(
        functools.partial(chunks_kernel, groups, tuple(len(a) for a in adds)),
        out_shape=[jax.ShapeDtypeStruct((g, rows, width), BF) for g in groups],
        grid_spec=pltpu.PrefetchScalarGridSpec(
            num_scalar_prefetch=1,
            grid=(rows // TILE,),
            in_specs=in_specs,
            out_specs=[pl.BlockSpec((g, TILE, width), lambda i, p: (0, i, 0)) for g in groups],
            scratch_shapes=[
                pltpu.VMEM((n, depth, width), BF),
                pltpu.SemaphoreType.DMA((n,)),
            ],
        ),
        compiler_params=params(),
        name="chunks",
    )(index, *operands)


def gather_order(x, y, c):
    way = 1 - 2 * c
    places = [(x, y, c), (x, y, 1 - c), (x, y - way, c), (x, y - way, 1 - c)]
    places += [(x, y + way, 1 - c), (x, y + way, c)]
    places += [(1 - x, y, c), (1 - x, y, 1 - c), (x, y + 2, c), (x, y + 2, 1 - c)]
    places += [(1 - x, y - way, c), (1 - x, y - way, 1 - c)]
    places += [(1 - x, y + way, 1 - c), (1 - x, y + way, c)]
    places += [(1 - x, y + 2, c), (1 - x, y + 2, 1 - c)]
    return jnp.stack(
        [side * 8 + (row + 4) % 4 * 2 + core for side, row, core in places]
    ).astype(jnp.int32)


def rotary_tables(position, member):
    lanes = jnp.arange(HD, dtype=jnp.int32)
    sign = jnp.where(lanes % 2 == 0, -1.0, 1.0).astype(F32)

    def table(pairs):
        frequency = jnp.exp(pairs.astype(F32) * (-2.0 * math.log(rope_base) / HD))
        angles = position.astype(F32)[:, None] * frequency[None, :]
        return jnp.cos(angles), jnp.sin(angles) * sign[None, :]

    q_cos, q_sin = table(lanes // 2)
    columns = member * HD + lanes
    kv_cos, kv_sin = table(columns // (2 * KVH) % (HD // 2))
    keys = member < KVH
    return q_cos, q_sin, jnp.where(keys, kv_cos, 1.0), jnp.where(keys, kv_sin, 0.0)


def body(rollout, lengths, target, w_query, w_keyval, w_out):
    member = lax.axis_index("tp")
    x, y, c = member // 8, member // 2 % 4, member % 2
    section_ids = jnp.arange(8, dtype=jnp.int32)
    own_lengths = lengths[0]
    chosen = target[0][None, :] == section_ids[:, None]
    before = jnp.cumsum(own_lengths) - own_lengths
    start_to = jnp.sum(jnp.where(chosen, before[None, :], 0), axis=1)
    sent_from = jnp.minimum(start_to // ALIGN * ALIGN, rollout.shape[0] - SENT)
    count_to = jnp.sum(jnp.where(chosen, own_lengths[None, :], 0), axis=1)
    facts = jnp.stack([count_to, start_to - sent_from], axis=1)
    outgoing = cut(rollout, sent_from)
    arrived = lax.all_to_all(outgoing, "sec", split_axis=0, concat_axis=0, tiled=True)
    facts = lax.all_to_all(facts, "sec", split_axis=0, concat_axis=0, tiled=True)
    counts, shifts = facts[:, 0], facts[:, 1]
    ends = jnp.cumsum(counts)
    offsets = ends - counts
    plan = jnp.stack([offsets, ends, shifts - offsets])
    row_ids = jnp.arange(CAP, dtype=jnp.int32)
    begin = jnp.max(
        jnp.where(row_ids[:, None] >= offsets[None, :], offsets[None, :], 0), axis=1
    )
    order = gather_order(x, y, c)
    weights = w_query[0], w_keyval[0]
    w_out = w_out[0]
    line = Line()
    way = 1 - 2 * c
    sides = (1 - x, x)

    def at(*places):
        return jnp.stack(
            [side * 8 + (row + 4) % 4 * 2 + core for side, row, core in places]
        ).astype(jnp.int32)

    def move(value, pairs):
        return send(line.next(value), pairs)

    def stack(*arrays):
        return line.add(jnp.stack([line.next(arrays[0]), *arrays[1:]]))

    def part(value, *index):
        return line.add(line.next(value)[index])

    def projected(pieces, index, *more):
        pieces = [p[None] for p in pieces]
        return line.add(project(pieces, line.next(index), *weights, *more))

    def spread(keyval):
        keyval = lax.all_to_all(
            line.next(keyval), "tp", split_axis=0, concat_axis=0, tiled=True
        )
        return keyval.reshape(2 * HD, BLOCK)

    def attended(block, query, keyvals):
        return line.add(attend(block, line.next(plan), query, keyvals))

    def join(*arrays):
        *arrays, line.last = lax.optimization_barrier((*arrays, line.last))
        return arrays

    def summed(heads, places, groups, adds):
        index = line.next(at(*places))
        return line.add(chunks(heads, w_out, index, groups, adds))

    def for_core(heads, places):
        parts = summed(heads, places, (1,) * len(places), [[]] * len(places))
        return [send(p, TO_CORE) for p in parts]

    def far_for_core(heads):
        return for_core(heads, [(side, y + 2, 1 - c) for side in sides])

    def near_for_core(heads):
        places = []
        for side in sides:
            places += [(side, y - way, 1 - c), (side, y - way, c)]
        return for_core(heads, places)

    def far_sums(heads, passed):
        places = [(side, y + 2, c) for side in sides]
        adds = [[(p, 0)] for p in passed]
        return send(summed(heads, places, (2,), adds)[0], TO_Y)

    def near_sums(heads, passed, far, groups):
        places, adds = [], []
        for i, side in enumerate(sides):
            places += [(side, y + way, c), (side, y + way, 1 - c)]
            adds += [[(passed[2 * i], 0), (far, i)], [(passed[2 * i + 1], 0)]]
        return summed(heads, places, groups, adds)

    def last_sum(i, heads, near, place, *more):
        shared = summed(heads, [(sides[i], y, 1 - c)], (1,), [[(near, place + 1)]])[0]
        terms = [(near, place), (send(shared, TO_CORE), 0)] + [(t, 0) for t in more]
        return summed(heads, [(sides[i], y, c)], (1,), [terms])[0]


    value = line.add(pack(arrived, plan))
    across = send(value, TO_X)
    up = send(value, TO_Y)
    other = send(value, TO_CORE)
    up_other = send(other, TO_Y)
    position = line.next(row_ids) - begin
    tables = line.add(rotary_tables(position, member))
    total = projected([value, other], order[:2], CAP)
    across, up, up_other = join(across, up, up_other)
    there_up1 = [send(u[BLOCK:], TO_X) for u in (up, up_other)]
    far = send(up, TO_Y)
    across_other = send(across, TO_CORE)
    there_up0 = [send(a[:BLOCK], TO_Y) for a in (across, across_other)]
    down, down_other = send(up, TO_CORE), send(up_other, TO_CORE)
    pieces = [up, up_other, down, down_other, across, across_other]
    total = projected(pieces, order[2:8], CAP, total)
    far, *there_up = join(far, *there_up0, *there_up1)
    there_far0 = send(there_up[0], TO_Y)
    there_far1 = send(far[BLOCK:], TO_X)
    far_other = send(far, TO_CORE)
    there_down = [send(u, TO_CORE) for u in there_up]
    pieces = [far, far_other, *there_up[:2], *there_down[:2]]
    total0 = projected(pieces, order[8:14], BLOCK, total, None, 0)
    there_far0, far = join(there_far0, far)
    pieces = [there_far0, send(there_far0, TO_CORE)]
    index = after(order[14:], there_far1)
    query0, keyval0 = projected(pieces, index, BLOCK, total0, tables, 0)
    keyval0 = spread(keyval0)
    pieces = [far, far_other, *there_up[2:], *there_down[2:]]
    pieces += [there_far1, move(there_far1, TO_CORE)]
    query1, keyval1 = projected(pieces, order[8:], BLOCK, total, tables, 1)
    keyval1 = spread(keyval1)

    heads0 = attended(0, query0, [keyval0])
    far0 = far_sums(heads0, far_for_core(heads0))
    heads1 = attended(1, query1, [keyval0, keyval1])
    far1 = far_sums(heads1, far_for_core(heads1))
    passed = near_for_core(heads0)
    near0 = [send(t, TO_Y) for t in near_sums(heads0, passed, far0, (2, 2))]
    passed = near_for_core(heads1)
    near1 = [send(t, TO_Y) for t in near_sums(heads1, passed, far1, (2, 2))]
    crossed0 = send(last_sum(0, heads0, near0[0], 0), TO_X)
    crossed1 = send(last_sum(0, heads1, near1[0], 0), TO_X)
    result0 = last_sum(1, heads0, near0[1], 0, crossed0)
    result1 = last_sum(1, heads1, near1[1], 0, crossed1)
    return jnp.concatenate([result0[0], result1[0]], axis=0)


def solution(mesh):
    placed = (
        P("sec", "tp"),
        P("sec", None),
        P("sec", None),
        P("sec", None, "tp"),
        P("sec", None, "tp"),
        P("sec", "tp", None),
    )
    return jax.shard_map(
        body, mesh=mesh, in_specs=placed, out_specs=P("sec", "tp"), check_vma=False
    )
```

```python
import functools
import math

import jax
import jax.numpy as jnp
from jax import lax
from jax.experimental import pallas as pl
from jax.experimental.pallas import tpu as pltpu
from jax.sharding import PartitionSpec as P

HQ = 64
KVH = 8
HD = 128
CAP = 1024
SLOT = 256
ALIGN = 16
SENT = SLOT + ALIGN
TILE = 256
BLOCK = 512
rope_base = 500000.0
BF = jnp.bfloat16
F32 = jnp.float32


def params():
    return pltpu.CompilerParams(vmem_limit_bytes=14 << 20)


def permutation(move):
    pairs = []
    for t in range(16):
        x, y, c = move(t // 8, t // 2 % 4, t % 2)
        pairs.append((t, x % 2 * 8 + y % 4 * 2 + c % 2))
    return pairs


TO_CORE = permutation(lambda x, y, c: (x, y, c + 1))
TO_X = permutation(lambda x, y, c: (x + 1, y, c))
TO_Y = permutation(lambda x, y, c: (x, y + 1 - 2 * c, c))


def after(value, *others):
    return lax.optimization_barrier((value, *others))[0]


class Line:
    def __init__(self):
        self.last = None

    def next(self, value):
        return value if self.last is None else after(value, self.last)

    def add(self, result):
        self.last = jax.tree.leaves(result)[0]
        return result


def send(value, pairs):
    return lax.ppermute(value, "tp", pairs)


def in_hbm(array):
    return pltpu.with_memory_space_constraint(array, pltpu.HBM)


def cut_kernel(start_ref, rollout_ref, sent_ref):
    for d in range(8):
        row = pl.multiple_of(start_ref[d], ALIGN)
        sent_ref[d] = rollout_ref[pl.ds(row, SENT), :]


def cut(rollout, starts):
    return pl.pallas_call(
        cut_kernel,
        out_shape=jax.ShapeDtypeStruct((8, SENT, rollout.shape[1]), BF),
        in_specs=[
            pl.BlockSpec(memory_space=pltpu.SMEM),
            pl.BlockSpec(memory_space=pltpu.VMEM),
        ],
        out_specs=pl.BlockSpec(memory_space=pltpu.VMEM),
        compiler_params=params(),
        name="cut",
    )(starts, rollout)


def pack_kernel(plan_ref, arrived_ref, packed_ref, total_ref):
    first = pl.program_id(0) * TILE
    rows = first + lax.broadcasted_iota(jnp.int32, (TILE, 1), 0)
    slots = lax.broadcasted_iota(jnp.int32, (TILE, SENT), 1)
    total_ref[...] = jnp.zeros_like(total_ref)
    for s in range(8):
        begin, end = plan_ref[0, s], plan_ref[1, s]

        @pl.when((begin < first + TILE) & (end > first))
        def _():
            source = jnp.where(
                (rows >= begin) & (rows < end), rows + plan_ref[2, s], -1
            )
            picked = jnp.where(slots == source, 1.0, 0.0).astype(BF)
            total_ref[...] += jnp.dot(
                picked, arrived_ref[s], preferred_element_type=F32
            )

    packed_ref[...] = total_ref[...].astype(BF)


def pack(arrived, plan):
    width = arrived.shape[2]
    return pl.pallas_call(
        pack_kernel,
        out_shape=jax.ShapeDtypeStruct((CAP, width), BF),
        grid_spec=pltpu.PrefetchScalarGridSpec(
            num_scalar_prefetch=1,
            grid=(CAP // TILE,),
            in_specs=[pl.BlockSpec(memory_space=pltpu.VMEM)],
            out_specs=pl.BlockSpec((TILE, width), lambda i, p: (i, 0)),
            scratch_shapes=[pltpu.VMEM((TILE, width), F32)],
        ),
        compiler_params=params(),
        name="pack",
    )(plan, arrived)


def swap_members(values):
    lanes = lax.broadcasted_iota(jnp.int32, values.shape, 1)
    return jnp.where(
        lanes % 2 == 0, pltpu.roll(values, HD - 1, 1), pltpu.roll(values, 1, 1)
    )


def heads_first(keyval):
    to = lax.broadcasted_iota(jnp.int32, (HD, HD), 0)
    came = lax.broadcasted_iota(jnp.int32, (HD, HD), 1)
    order = jnp.where(came == to % 16 // 2 * 16 + to // 16 * 2 + to % 2, 1.0, 0.0).astype(BF)
    return lax.dot_general(
        order, keyval, (((1,), (1,)), ((), ())), preferred_element_type=F32
    ).astype(BF)


def project_kernel(counts, has_total, last, index_ref, *refs):
    refs = list(refs)
    pieces = [refs.pop(0) for _ in counts]
    query_w, keyval_w = refs.pop(0), refs.pop(0)
    total_ref = refs.pop(0) if has_total else None
    tables = [refs.pop(0) for _ in range(4)] if last else None
    weights_ref, sems = refs[-2:]
    refs = refs[:-2]
    columns = query_w.shape[1]
    depth = pieces[0].shape[2]
    copies = []
    for k in range(sum(counts)):
        rows = pl.ds(pl.multiple_of(index_ref[k] * depth, depth), depth)
        copies.append((
            pltpu.make_async_copy(
                query_w.at[rows, :], weights_ref.at[k, :, pl.ds(0, columns)], sems.at[k, 0]
            ),
            pltpu.make_async_copy(
                keyval_w.at[rows, :], weights_ref.at[k, :, pl.ds(columns, HD)], sems.at[k, 1]
            ),
        ))

    @pl.when(pl.program_id(0) == 0)
    def _():
        for pair in copies:
            for copy in pair:
                copy.start()

    query = total_ref[:, :columns] if has_total else 0.0
    keyval = total_ref[:, columns:] if has_total else 0.0
    k = 0
    for ref, count in zip(pieces, counts):
        for j in range(count):

            @pl.when(pl.program_id(0) == 0)
            def _(k=k):
                for copy in copies[k]:
                    copy.wait()

            left = ref[j]
            query += jnp.dot(left, weights_ref[k, :, :columns], preferred_element_type=F32)
            keyval += jnp.dot(left, weights_ref[k, :, columns:], preferred_element_type=F32)
            k += 1
    if not last:
        refs[0][:, :columns] = query
        refs[0][:, columns:] = keyval
        return
    query_out, keyval_out = refs
    q_cos, q_sin, kv_cos, kv_sin = [t[...] for t in tables]
    for head in range(columns // HD):
        span = slice(head * HD, (head + 1) * HD)
        part = query[:, span]
        query_out[:, span] = (part * q_cos + swap_members(part) * q_sin).astype(BF)
    turned = (keyval * kv_cos + swap_members(keyval) * kv_sin).astype(BF)
    turned = heads_first(turned)
    for member in range(2 * KVH):
        keyval_out[member] = turned[member // 2 * 16 : member // 2 * 16 + 16]


def project(pieces, index, w_query, w_keyval, rows, total=None, tables=None, block=0):
    counts = tuple(p.shape[0] for p in pieces)
    n = sum(counts)
    width = pieces[0].shape[2]
    columns = w_query.shape[1]
    last = tables is not None

    def skip(array, axis):
        return block * (BLOCK // TILE) if array.shape[axis] > rows else 0

    in_specs = [
        pl.BlockSpec((p.shape[0], TILE, width), lambda i, _, at=skip(p, 1): (0, i + at, 0))
        for p in pieces
    ]
    in_specs += [pl.BlockSpec(memory_space=pltpu.HBM)] * 2
    operands = list(pieces) + [in_hbm(w_query), in_hbm(w_keyval)]
    if total is not None:
        at = skip(total, 0)
        in_specs.append(pl.BlockSpec((TILE, columns + HD), lambda i, _: (i + at, 0)))
        operands.append(in_hbm(total))
    if last:
        first = skip(tables[0], 0)
        in_specs += [pl.BlockSpec((TILE, HD), lambda i, _: (i + first, 0))] * 4
        operands += [in_hbm(t) for t in tables]
        out_shape = (
            jax.ShapeDtypeStruct((rows, columns), BF),
            jax.ShapeDtypeStruct((2 * KVH, 16, rows), BF),
        )
        out_specs = [
            pl.BlockSpec((TILE, columns), lambda i, _: (i, 0)),
            pl.BlockSpec((2 * KVH, 16, TILE), lambda i, _: (0, 0, i)),
        ]
    else:
        out_shape = jax.ShapeDtypeStruct((rows, columns + HD), F32)
        out_specs = pl.BlockSpec((TILE, columns + HD), lambda i, _: (i, 0))
    return pl.pallas_call(
        functools.partial(project_kernel, counts, total is not None, last),
        out_shape=out_shape,
        grid_spec=pltpu.PrefetchScalarGridSpec(
            num_scalar_prefetch=1,
            grid=(rows // TILE,),
            in_specs=in_specs,
            out_specs=out_specs,
            scratch_shapes=[
                pltpu.VMEM((n, width, columns + HD), BF),
                pltpu.SemaphoreType.DMA((n, 2)),
            ],
        ),
        compiler_params=params(),
        name="project",
    )(index, *operands)


def project_block_kernel(skips, last, index_ref, *refs):
    refs = list(refs)
    n = len(skips) - 2
    pieces = [refs.pop(0) for _ in range(n)]
    query_w, keyval_w, total = refs.pop(0), refs.pop(0), refs.pop(0)
    tables = [refs.pop(0) for _ in range(4)] if last else []
    *outs, left_ref, weights_ref, sum_ref, table_ref, sems = refs
    depth, columns = left_ref.shape[2], query_w.shape[1]
    copy = pltpu.make_async_copy
    fetches = []
    for k, piece in enumerate(pieces):
        rows = pl.ds(pl.multiple_of(index_ref[k] * depth, depth), depth)
        fetches.append([
            copy(piece.at[pl.ds(skips[k], BLOCK), :], left_ref.at[k], sems.at[k, 0]),
            copy(query_w.at[rows, :], weights_ref.at[k, :, pl.ds(0, columns)], sems.at[k, 1]),
            copy(keyval_w.at[rows, :], weights_ref.at[k, :, pl.ds(columns, HD)], sems.at[k, 2]),
        ])
    fetch_total = copy(total.at[pl.ds(skips[n], BLOCK), :], sum_ref, sems.at[n, 0])
    fetch_tables = [
        copy(table.at[pl.ds(skips[n + 1], BLOCK), :], table_ref.at[j], sems.at[n + 1, j])
        for j, table in enumerate(tables)
    ]
    for fetch in [*fetches[0], fetch_total, *sum(fetches[1:], []), *fetch_tables]:
        fetch.start()
    for k in range(n):
        for fetch in fetches[k]:
            fetch.wait()
        if k == 0:
            fetch_total.wait()
        for tile in range(BLOCK // TILE):
            rows = slice(tile * TILE, (tile + 1) * TILE)
            left = left_ref[k, rows, :]
            for span in (slice(0, columns), slice(columns, columns + HD)):
                sum_ref[rows, span] += jnp.dot(
                    left, weights_ref[k, :, span], preferred_element_type=F32
                )
    for fetch in fetch_tables:
        fetch.wait()
    if not last:
        outs[0][...] = sum_ref[...]
        return
    query_out, keyval_out = outs
    for tile in range(BLOCK // TILE):
        rows = slice(tile * TILE, (tile + 1) * TILE)
        q_cos, q_sin, kv_cos, kv_sin = [table_ref[j, rows, :] for j in range(4)]
        for head in range(columns // HD):
            span = slice(head * HD, (head + 1) * HD)
            part = sum_ref[rows, span]
            query_out[rows, span] = (part * q_cos + swap_members(part) * q_sin).astype(BF)
        part = sum_ref[rows, columns:]
        turned = heads_first((part * kv_cos + swap_members(part) * kv_sin).astype(BF))
        for member in range(2 * KVH):
            keyval_out[member, :, rows] = turned[member // 2 * 16 : member // 2 * 16 + 16]


def project_block(pieces, index, w_query, w_keyval, block, total, tables=()):
    n = len(pieces)
    width, columns = pieces[0].shape[1], w_query.shape[1]
    last = len(tables) > 0
    skips = [
        block * BLOCK if a.shape[0] > BLOCK else 0 for a in (*pieces, total, *tables[:1])
    ]
    if not last:
        skips.append(0)
    operands = [in_hbm(a) for a in (*pieces, w_query, w_keyval, total, *tables)]
    if last:
        out_shape = (
            jax.ShapeDtypeStruct((BLOCK, columns), BF),
            jax.ShapeDtypeStruct((2 * KVH, 16, BLOCK), BF),
        )
    else:
        out_shape = (jax.ShapeDtypeStruct((BLOCK, columns + HD), F32),)
    return pl.pallas_call(
        functools.partial(project_block_kernel, tuple(skips), last),
        out_shape=out_shape,
        in_specs=[pl.BlockSpec(memory_space=pltpu.SMEM)]
        + [pl.BlockSpec(memory_space=pltpu.HBM)] * len(operands),
        out_specs=[pl.BlockSpec(memory_space=pltpu.VMEM)] * len(out_shape),
        scratch_shapes=[
            pltpu.VMEM((n, BLOCK, width), BF),
            pltpu.VMEM((n, width, columns + HD), BF),
            pltpu.VMEM((BLOCK, columns + HD), F32),
            pltpu.VMEM((4, BLOCK, HD), F32),
            pltpu.SemaphoreType.DMA((n + 2, 4)),
        ],
        compiler_params=params(),
        name="project_block",
    )(index, *operands)


def attend_kernel(block, plan_ref, query_ref, *refs):
    keyval_refs, heads_ref = refs[:-1], refs[-1]
    scale = 1.0 / math.sqrt(HD)
    local_heads = query_ref.shape[1] // HD

    def columns_of(there, member):
        part, first = there * TILE // BLOCK, there * TILE % BLOCK
        return keyval_refs[part][member * HD : (member + 1) * HD, first : first + TILE]

    for tile in range(BLOCK // TILE):
        here = block * (BLOCK // TILE) + tile
        rows = here * TILE + lax.broadcasted_iota(jnp.int32, (TILE, 1), 0)
        begin = jnp.zeros((TILE, 1), jnp.int32)
        for s in range(8):
            begin = jnp.where(rows >= plan_ref[0, s], plan_ref[0, s], begin)
        filled = rows < plan_ref[1, 7]
        seen = []
        for there in range(max(here - 1, 0), here + 1):
            columns = there * TILE + lax.broadcasted_iota(jnp.int32, (TILE, TILE), 1)
            allowed = (columns >= begin) & (columns <= rows)
            seen.append((allowed, columns_of(there, 0), columns_of(there, 1)))
        for head in range(local_heads):
            span = slice(head * HD, (head + 1) * HD)
            query = query_ref[tile * TILE : (tile + 1) * TILE, span]
            scores = []
            for allowed, key, _ in seen:
                raw = jnp.dot(query, key, preferred_element_type=F32)
                scores.append(jnp.where(allowed, raw * scale, -1e30))
            top = functools.reduce(
                jnp.maximum, [jnp.max(s, axis=1, keepdims=True) for s in scores]
            )
            shifted = [jnp.exp(s - top) for s in scores]
            norm = sum(jnp.sum(s, axis=1, keepdims=True) for s in shifted)
            result = jnp.zeros((TILE, HD), F32)
            for part, (_, _, value) in zip(shifted, seen):
                weights = (part / norm).astype(BF)
                result += lax.dot_general(
                    weights, value, (((1,), (1,)), ((), ())), preferred_element_type=F32
                )
            heads_ref[tile * TILE : (tile + 1) * TILE, span] = jnp.where(
                filled, result, 0.0
            ).astype(BF)


def attend(block, plan, query, keyvals):
    return pl.pallas_call(
        functools.partial(attend_kernel, block),
        out_shape=jax.ShapeDtypeStruct(query.shape, BF),
        in_specs=[
            pl.BlockSpec(memory_space=pltpu.SMEM),
            pl.BlockSpec(memory_space=pltpu.VMEM),
        ]
        + [pl.BlockSpec(memory_space=pltpu.VMEM)] * len(keyvals),
        out_specs=pl.BlockSpec(memory_space=pltpu.VMEM),
        compiler_params=params(),
        name="attend",
    )(plan, query, *keyvals)


def chunks_kernel(groups, adds, index_ref, heads_ref, w_out, *refs):
    n = len(adds)
    refs = list(refs)
    weights_ref, sems = refs[-2:]
    outs = refs[-2 - len(groups) : -2]
    width = weights_ref.shape[2]
    copies = []
    for k in range(n):
        columns = pl.ds(pl.multiple_of(index_ref[k] * width, width), width)
        copies.append(
            pltpu.make_async_copy(w_out.at[:, columns], weights_ref.at[k], sems.at[k])
        )

    @pl.when(pl.program_id(0) == 0)
    def _():
        for copy in copies:
            copy.start()

    k = 0
    for out, size in zip(outs, groups):
        for j in range(size):

            @pl.when(pl.program_id(0) == 0)
            def _(k=k):
                copies[k].wait()

            total = jnp.dot(heads_ref[...], weights_ref[k], preferred_element_type=F32)
            for _ in range(adds[k]):
                total += refs.pop(0)[0].astype(F32)
            out[j] = total.astype(BF)
            k += 1


def chunks(heads, w_out, index, groups, adds, block=None, into=None):
    rows, depth = heads.shape
    width = 512
    n = len(adds)
    in_specs = [
        pl.BlockSpec((TILE, depth), lambda i, p: (i, 0)),
        pl.BlockSpec(memory_space=pltpu.HBM),
    ]
    operands = [heads, in_hbm(w_out)]
    for terms in adds:
        for array, place in terms:
            in_specs.append(
                pl.BlockSpec((1, TILE, width), lambda i, p, at=place: (at, i, 0))
            )
            operands.append(array)
    first = 0 if block is None else block * (BLOCK // TILE)
    out_rows = rows if block is None else CAP
    aliases = {}
    if into is not None:
        in_specs.append(pl.BlockSpec(memory_space=pl.ANY))
        operands.append(into)
        aliases = {len(operands): 0}
    return pl.pallas_call(
        functools.partial(chunks_kernel, groups, tuple(len(a) for a in adds)),
        input_output_aliases=aliases,
        out_shape=[jax.ShapeDtypeStruct((g, out_rows, width), BF) for g in groups],
        grid_spec=pltpu.PrefetchScalarGridSpec(
            num_scalar_prefetch=1,
            grid=(rows // TILE,),
            in_specs=in_specs,
            out_specs=[
                pl.BlockSpec((g, TILE, width), lambda i, p: (0, i + first, 0)) for g in groups
            ],
            scratch_shapes=[
                pltpu.VMEM((n, depth, width), BF),
                pltpu.SemaphoreType.DMA((n,)),
            ],
        ),
        compiler_params=params(),
        name="chunks",
    )(index, *operands)


def gather_order(x, y, c):
    way = 1 - 2 * c
    places = [(x, y, c), (x, y, 1 - c), (x, y - way, c), (x, y - way, 1 - c)]
    places += [(x, y + way, 1 - c), (x, y + way, c)]
    places += [(1 - x, y, c), (1 - x, y, 1 - c), (x, y + 2, c), (x, y + 2, 1 - c)]
    places += [(1 - x, y - way, c), (1 - x, y - way, 1 - c)]
    places += [(1 - x, y + way, 1 - c), (1 - x, y + way, c)]
    places += [(1 - x, y + 2, c), (1 - x, y + 2, 1 - c)]
    return jnp.stack(
        [side * 8 + (row + 4) % 4 * 2 + core for side, row, core in places]
    ).astype(jnp.int32)


def rotary_tables(position, member):
    lanes = jnp.arange(HD, dtype=jnp.int32)
    sign = jnp.where(lanes % 2 == 0, -1.0, 1.0).astype(F32)

    def table(pairs):
        frequency = jnp.exp(pairs.astype(F32) * (-2.0 * math.log(rope_base) / HD))
        angles = position.astype(F32)[:, None] * frequency[None, :]
        return jnp.cos(angles), jnp.sin(angles) * sign[None, :]

    q_cos, q_sin = table(lanes // 2)
    columns = member * HD + lanes
    kv_cos, kv_sin = table(columns // (2 * KVH) % (HD // 2))
    keys = member < KVH
    return q_cos, q_sin, jnp.where(keys, kv_cos, 1.0), jnp.where(keys, kv_sin, 0.0)


def body(rollout, lengths, target, w_query, w_keyval, w_out):
    member = lax.axis_index("tp")
    x, y, c = member // 8, member // 2 % 4, member % 2
    section_ids = jnp.arange(8, dtype=jnp.int32)
    own_lengths = lengths[0]
    chosen = target[0][None, :] == section_ids[:, None]
    before = jnp.cumsum(own_lengths) - own_lengths
    start_to = jnp.sum(jnp.where(chosen, before[None, :], 0), axis=1)
    sent_from = jnp.minimum(start_to // ALIGN * ALIGN, rollout.shape[0] - SENT)
    count_to = jnp.sum(jnp.where(chosen, own_lengths[None, :], 0), axis=1)
    facts = jnp.stack([count_to, start_to - sent_from], axis=1)
    outgoing = cut(rollout, sent_from)
    arrived = lax.all_to_all(outgoing, "sec", split_axis=0, concat_axis=0, tiled=True)
    facts = lax.all_to_all(facts, "sec", split_axis=0, concat_axis=0, tiled=True)
    counts, shifts = facts[:, 0], facts[:, 1]
    ends = jnp.cumsum(counts)
    offsets = ends - counts
    plan = jnp.stack([offsets, ends, shifts - offsets])
    row_ids = jnp.arange(CAP, dtype=jnp.int32)
    begin = jnp.max(
        jnp.where(row_ids[:, None] >= offsets[None, :], offsets[None, :], 0), axis=1
    )
    order = gather_order(x, y, c)
    weights = w_query[0], w_keyval[0]
    w_out = w_out[0]
    line = Line()
    way = 1 - 2 * c
    sides = (1 - x, x)

    def at(*places):
        return jnp.stack(
            [side * 8 + (row + 4) % 4 * 2 + core for side, row, core in places]
        ).astype(jnp.int32)

    def move(value, pairs):
        return send(line.next(value), pairs)

    def stack(*arrays):
        return line.add(jnp.stack([line.next(arrays[0]), *arrays[1:]]))

    def part(value, *index):
        return line.add(line.next(value)[index])

    def projected(pieces, index, *more):
        pieces = [p[None] for p in pieces]
        return line.add(project(pieces, line.next(index), *weights, *more))

    def projected_block(pieces, index, *more):
        return line.add(project_block(pieces, line.next(index), *weights, *more))

    def spread(keyval):
        keyval = lax.all_to_all(
            line.next(keyval), "tp", split_axis=0, concat_axis=0, tiled=True
        )
        return keyval.reshape(2 * HD, BLOCK)

    def attended(block, query, keyvals):
        return line.add(attend(block, line.next(plan), query, keyvals))

    def join(*arrays):
        *arrays, line.last = lax.optimization_barrier((*arrays, line.last))
        return arrays

    def summed(heads, places, groups, adds, **where):
        index = line.next(at(*places))
        return line.add(chunks(heads, w_out, index, groups, adds, **where))

    def for_core(heads, places):
        parts = summed(heads, places, (1,) * len(places), [[]] * len(places))
        return [send(p, TO_CORE) for p in parts]

    def far_for_core(heads):
        return for_core(heads, [(side, y + 2, 1 - c) for side in sides])

    def near_for_core(heads):
        places = []
        for side in sides:
            places += [(side, y - way, 1 - c), (side, y - way, c)]
        return for_core(heads, places)

    def far_sums(heads, passed):
        places = [(side, y + 2, c) for side in sides]
        adds = [[(p, 0)] for p in passed]
        return send(summed(heads, places, (2,), adds)[0], TO_Y)

    def near_sums(heads, passed, far, groups):
        places, adds = [], []
        for i, side in enumerate(sides):
            places += [(side, y + way, c), (side, y + way, 1 - c)]
            adds += [[(passed[2 * i], 0), (far, i)], [(passed[2 * i + 1], 0)]]
        return summed(heads, places, groups, adds)

    def last_sum(i, heads, near, *more, wait=None, **where):
        shared = summed(heads, [(sides[i], y, 1 - c)], (1,), [[(near, 1)]])[0]
        if wait is not None:
            near = after(near, wait)
        terms = [(t, 0) for t in (near, send(shared, TO_CORE), *more)]
        return summed(heads, [(sides[i], y, c)], (1,), [terms], **where)[0]


    value = line.add(pack(arrived, plan))
    across = send(value, TO_X)
    up = send(value, TO_Y)
    other = send(value, TO_CORE)
    up_other = send(other, TO_Y)
    position = line.next(row_ids) - begin
    tables = line.add(rotary_tables(position, member))
    total = projected([value, other, up], order[:3], CAP)
    across, up_other = join(across, up_other)
    there_up1 = [send(u[BLOCK:], TO_X) for u in (up, up_other)]
    far = send(up, TO_Y)
    across_other = send(across, TO_CORE)
    there_up0 = [send(a[:BLOCK], TO_Y) for a in (across, across_other)]
    down, down_other = send(up, TO_CORE), send(up_other, TO_CORE)
    pieces = [up_other, down, down_other, across, across_other]
    total = projected(pieces, order[3:8], CAP, total)
    far_high = after(far, total)[BLOCK:]
    far, far_high, *there_up = join(far, far_high, *there_up0, *there_up1)
    there_far0 = send(there_up[0], TO_Y)
    there_far1 = send(far_high, TO_X)
    far_other = send(far, TO_CORE)
    there_down = [send(u, TO_CORE) for u in there_up]
    pieces = [far, far_other, *there_up[:2], *there_down[:2]]
    total0 = projected_block(pieces, order[8:14], 0, total)[0]
    there_far0, far = join(there_far0, far)
    pieces = [there_far0, send(there_far0, TO_CORE)]
    index = after(order[14:], there_far1)
    query0, keyval0 = projected_block(pieces, index, 0, total0, tables)
    keyval0 = spread(keyval0)
    pieces = [far, far_other, *there_up[2:], *there_down[2:]]
    pieces += [there_far1, move(there_far1, TO_CORE)]
    query1, keyval1 = projected_block(pieces, order[8:], 1, total, tables)
    keyval1 = spread(keyval1)

    heads0 = attended(0, query0, [keyval0])
    far0 = far_sums(heads0, far_for_core(heads0))
    heads1 = attended(1, query1, [keyval0, keyval1])
    far1 = far_sums(heads1, far_for_core(heads1))
    passed = near_for_core(heads0)
    near0 = [send(t, TO_Y) for t in near_sums(heads0, passed, far0, (2, 2))]
    passed = near_for_core(heads1)
    near1 = [send(t, TO_Y) for t in near_sums(heads1, passed, far1, (2, 2))]
    crossed0 = send(last_sum(0, heads0, near0[0]), TO_X)
    crossed1 = send(last_sum(0, heads1, near1[0], wait=crossed0), TO_X)
    result = last_sum(1, heads0, near0[1], crossed0, block=0)
    return last_sum(1, heads1, near1[1], crossed1, block=1, into=result)[0]


def solution(mesh):
    placed = (
        P("sec", "tp"),
        P("sec", None),
        P("sec", None),
        P("sec", None, "tp"),
        P("sec", None, "tp"),
        P("sec", "tp", None),
    )
    return jax.shard_map(
        body, mesh=mesh, in_specs=placed, out_specs=P("sec", "tp"), check_vma=False
    )
```

```python
import functools
import math

import jax
import jax.numpy as jnp
from jax import lax
from jax.experimental import pallas as pl
from jax.experimental.pallas import tpu as pltpu
from jax.sharding import PartitionSpec as P

HQ = 64
KVH = 8
HD = 128
CAP = 1024
SLOT = 256
ALIGN = 16
SENT = SLOT + ALIGN
TILE = 256
BLOCK = 512
rope_base = 500000.0
BF = jnp.bfloat16
F32 = jnp.float32


def params():
    return pltpu.CompilerParams(vmem_limit_bytes=14 << 20)


def permutation(move):
    pairs = []
    for t in range(16):
        x, y, c = move(t // 8, t // 2 % 4, t % 2)
        pairs.append((t, x % 2 * 8 + y % 4 * 2 + c % 2))
    return pairs


TO_CORE = permutation(lambda x, y, c: (x, y, c + 1))
TO_X = permutation(lambda x, y, c: (x + 1, y, c))
TO_Y = permutation(lambda x, y, c: (x, y + 1 - 2 * c, c))


def after(value, *others):
    return lax.optimization_barrier((value, *others))[0]


class Line:
    def __init__(self):
        self.last = None

    def next(self, value):
        return value if self.last is None else after(value, self.last)

    def add(self, result):
        self.last = jax.tree.leaves(result)[0]
        return result


def send(value, pairs):
    return lax.ppermute(value, "tp", pairs)


def in_hbm(array):
    return pltpu.with_memory_space_constraint(array, pltpu.HBM)


def cut_kernel(start_ref, rollout_ref, sent_ref):
    for d in range(8):
        row = pl.multiple_of(start_ref[d], ALIGN)
        sent_ref[d] = rollout_ref[pl.ds(row, SENT), :]


def cut(rollout, starts):
    return pl.pallas_call(
        cut_kernel,
        out_shape=jax.ShapeDtypeStruct((8, SENT, rollout.shape[1]), BF),
        in_specs=[
            pl.BlockSpec(memory_space=pltpu.SMEM),
            pl.BlockSpec(memory_space=pltpu.VMEM),
        ],
        out_specs=pl.BlockSpec(memory_space=pltpu.VMEM),
        compiler_params=params(),
        name="cut",
    )(starts, rollout)


def pack_kernel(plan_ref, arrived_ref, packed_ref, total_ref):
    first = pl.program_id(0) * TILE
    rows = first + lax.broadcasted_iota(jnp.int32, (TILE, 1), 0)
    slots = lax.broadcasted_iota(jnp.int32, (TILE, SENT), 1)
    total_ref[...] = jnp.zeros_like(total_ref)

    @pl.loop(0, 8)
    def _(s):
        begin, end = plan_ref[0, s], plan_ref[1, s]

        @pl.when((begin < first + TILE) & (end > first))
        def _():
            source = jnp.where(
                (rows >= begin) & (rows < end), rows + plan_ref[2, s], -1
            )
            picked = jnp.where(slots == source, 1.0, 0.0).astype(BF)
            total_ref[...] += jnp.dot(
                picked, arrived_ref[s], preferred_element_type=F32
            )

    packed_ref[...] = total_ref[...].astype(BF)


def pack(arrived, plan):
    width = arrived.shape[2]
    return pl.pallas_call(
        pack_kernel,
        out_shape=jax.ShapeDtypeStruct((CAP, width), BF),
        grid_spec=pltpu.PrefetchScalarGridSpec(
            num_scalar_prefetch=1,
            grid=(CAP // TILE,),
            in_specs=[pl.BlockSpec(memory_space=pltpu.VMEM)],
            out_specs=pl.BlockSpec((TILE, width), lambda i, p: (i, 0)),
            scratch_shapes=[pltpu.VMEM((TILE, width), F32)],
        ),
        compiler_params=params(),
        name="pack",
    )(plan, arrived)


def swap_members(values):
    lanes = lax.broadcasted_iota(jnp.int32, values.shape, 1)
    return jnp.where(
        lanes % 2 == 0, pltpu.roll(values, HD - 1, 1), pltpu.roll(values, 1, 1)
    )


def heads_first(keyval):
    to = lax.broadcasted_iota(jnp.int32, (HD, HD), 0)
    came = lax.broadcasted_iota(jnp.int32, (HD, HD), 1)
    order = jnp.where(came == to % 16 // 2 * 16 + to // 16 * 2 + to % 2, 1.0, 0.0).astype(BF)
    return lax.dot_general(
        order, keyval, (((1,), (1,)), ((), ())), preferred_element_type=F32
    ).astype(BF)


def project_kernel(counts, has_total, last, index_ref, *refs):
    refs = list(refs)
    pieces = [refs.pop(0) for _ in counts]
    query_w, keyval_w = refs.pop(0), refs.pop(0)
    total_ref = refs.pop(0) if has_total else None
    tables = [refs.pop(0) for _ in range(4)] if last else None
    weights_ref, sems = refs[-2:]
    refs = refs[:-2]
    columns = query_w.shape[1]
    depth = pieces[0].shape[2]
    copies = []
    for k in range(sum(counts)):
        rows = pl.ds(pl.multiple_of(index_ref[k] * depth, depth), depth)
        copies.append((
            pltpu.make_async_copy(
                query_w.at[rows, :], weights_ref.at[k, :, pl.ds(0, columns)], sems.at[k, 0]
            ),
            pltpu.make_async_copy(
                keyval_w.at[rows, :], weights_ref.at[k, :, pl.ds(columns, HD)], sems.at[k, 1]
            ),
        ))

    @pl.when(pl.program_id(0) == 0)
    def _():
        for pair in copies:
            for copy in pair:
                copy.start()

    query = total_ref[:, :columns] if has_total else 0.0
    keyval = total_ref[:, columns:] if has_total else 0.0
    k = 0
    for ref, count in zip(pieces, counts):
        for j in range(count):

            @pl.when(pl.program_id(0) == 0)
            def _(k=k):
                for copy in copies[k]:
                    copy.wait()

            left = ref[j]
            query += jnp.dot(left, weights_ref[k, :, :columns], preferred_element_type=F32)
            keyval += jnp.dot(left, weights_ref[k, :, columns:], preferred_element_type=F32)
            k += 1
    if not last:
        refs[0][:, :columns] = query
        refs[0][:, columns:] = keyval
        return
    query_out, keyval_out = refs
    q_cos, q_sin, kv_cos, kv_sin = [t[...] for t in tables]
    for head in range(columns // HD):
        span = slice(head * HD, (head + 1) * HD)
        part = query[:, span]
        query_out[:, span] = (part * q_cos + swap_members(part) * q_sin).astype(BF)
    turned = (keyval * kv_cos + swap_members(keyval) * kv_sin).astype(BF)
    turned = heads_first(turned)
    for member in range(2 * KVH):
        keyval_out[member] = turned[member // 2 * 16 : member // 2 * 16 + 16]


def project(pieces, index, w_query, w_keyval, rows, total=None, tables=None, block=0):
    counts = tuple(p.shape[0] for p in pieces)
    n = sum(counts)
    width = pieces[0].shape[2]
    columns = w_query.shape[1]
    last = tables is not None

    def skip(array, axis):
        return block * (BLOCK // TILE) if array.shape[axis] > rows else 0

    in_specs = [
        pl.BlockSpec((p.shape[0], TILE, width), lambda i, _, at=skip(p, 1): (0, i + at, 0))
        for p in pieces
    ]
    in_specs += [pl.BlockSpec(memory_space=pltpu.HBM)] * 2
    operands = list(pieces) + [in_hbm(w_query), in_hbm(w_keyval)]
    if total is not None:
        at = skip(total, 0)
        in_specs.append(pl.BlockSpec((TILE, columns + HD), lambda i, _: (i + at, 0)))
        operands.append(in_hbm(total))
    if last:
        first = skip(tables[0], 0)
        in_specs += [pl.BlockSpec((TILE, HD), lambda i, _: (i + first, 0))] * 4
        operands += [in_hbm(t) for t in tables]
        out_shape = (
            jax.ShapeDtypeStruct((rows, columns), BF),
            jax.ShapeDtypeStruct((2 * KVH, 16, rows), BF),
        )
        out_specs = [
            pl.BlockSpec((TILE, columns), lambda i, _: (i, 0)),
            pl.BlockSpec((2 * KVH, 16, TILE), lambda i, _: (0, 0, i)),
        ]
    else:
        out_shape = jax.ShapeDtypeStruct((rows, columns + HD), F32)
        out_specs = pl.BlockSpec((TILE, columns + HD), lambda i, _: (i, 0))
    return pl.pallas_call(
        functools.partial(project_kernel, counts, total is not None, last),
        out_shape=out_shape,
        grid_spec=pltpu.PrefetchScalarGridSpec(
            num_scalar_prefetch=1,
            grid=(rows // TILE,),
            in_specs=in_specs,
            out_specs=out_specs,
            scratch_shapes=[
                pltpu.VMEM((n, width, columns + HD), BF),
                pltpu.SemaphoreType.DMA((n, 2)),
            ],
        ),
        compiler_params=params(),
        name="project",
    )(index, *operands)


def project_block_kernel(skips, last, index_ref, *refs):
    refs = list(refs)
    n = len(skips) - 2
    pieces = [refs.pop(0) for _ in range(n)]
    query_w, keyval_w, total = refs.pop(0), refs.pop(0), refs.pop(0)
    tables = [refs.pop(0) for _ in range(4)] if last else []
    *outs, left_ref, weights_ref, sum_ref, table_ref, sems = refs
    depth, columns = left_ref.shape[2], query_w.shape[1]
    copy = pltpu.make_async_copy
    fetches = []
    for k, piece in enumerate(pieces):
        rows = pl.ds(pl.multiple_of(index_ref[k] * depth, depth), depth)
        fetches.append([
            copy(piece.at[pl.ds(skips[k], BLOCK), :], left_ref.at[k], sems.at[k, 0]),
            copy(query_w.at[rows, :], weights_ref.at[k, :, pl.ds(0, columns)], sems.at[k, 1]),
            copy(keyval_w.at[rows, :], weights_ref.at[k, :, pl.ds(columns, HD)], sems.at[k, 2]),
        ])
    fetch_total = copy(total.at[pl.ds(skips[n], BLOCK), :], sum_ref, sems.at[n, 0])
    fetch_tables = [
        copy(table.at[pl.ds(skips[n + 1], BLOCK), :], table_ref.at[j], sems.at[n + 1, j])
        for j, table in enumerate(tables)
    ]
    for fetch in [*fetches[0], fetch_total, *sum(fetches[1:], []), *fetch_tables]:
        fetch.start()
    for k in range(n):
        for fetch in fetches[k]:
            fetch.wait()
        if k == 0:
            fetch_total.wait()
        for tile in range(BLOCK // TILE):
            rows = slice(tile * TILE, (tile + 1) * TILE)
            left = left_ref[k, rows, :]
            for span in (slice(0, columns), slice(columns, columns + HD)):
                sum_ref[rows, span] += jnp.dot(
                    left, weights_ref[k, :, span], preferred_element_type=F32
                )
    for fetch in fetch_tables:
        fetch.wait()
    if not last:
        outs[0][...] = sum_ref[...]
        return
    query_out, keyval_out = outs
    for tile in range(BLOCK // TILE):
        rows = slice(tile * TILE, (tile + 1) * TILE)
        q_cos, q_sin, kv_cos, kv_sin = [table_ref[j, rows, :] for j in range(4)]
        for head in range(columns // HD):
            span = slice(head * HD, (head + 1) * HD)
            part = sum_ref[rows, span]
            query_out[rows, span] = (part * q_cos + swap_members(part) * q_sin).astype(BF)
        part = sum_ref[rows, columns:]
        turned = heads_first((part * kv_cos + swap_members(part) * kv_sin).astype(BF))
        for member in range(2 * KVH):
            keyval_out[member, :, rows] = turned[member // 2 * 16 : member // 2 * 16 + 16]


def project_block(pieces, index, w_query, w_keyval, block, total, tables=()):
    n = len(pieces)
    width, columns = pieces[0].shape[1], w_query.shape[1]
    last = len(tables) > 0
    skips = [
        block * BLOCK if a.shape[0] > BLOCK else 0 for a in (*pieces, total, *tables[:1])
    ]
    if not last:
        skips.append(0)
    operands = [in_hbm(a) for a in (*pieces, w_query, w_keyval, total, *tables)]
    if last:
        out_shape = (
            jax.ShapeDtypeStruct((BLOCK, columns), BF),
            jax.ShapeDtypeStruct((2 * KVH, 16, BLOCK), BF),
        )
    else:
        out_shape = (jax.ShapeDtypeStruct((BLOCK, columns + HD), F32),)
    return pl.pallas_call(
        functools.partial(project_block_kernel, tuple(skips), last),
        out_shape=out_shape,
        in_specs=[pl.BlockSpec(memory_space=pltpu.SMEM)]
        + [pl.BlockSpec(memory_space=pltpu.HBM)] * len(operands),
        out_specs=[pl.BlockSpec(memory_space=pltpu.VMEM)] * len(out_shape),
        scratch_shapes=[
            pltpu.VMEM((n, BLOCK, width), BF),
            pltpu.VMEM((n, width, columns + HD), BF),
            pltpu.VMEM((BLOCK, columns + HD), F32),
            pltpu.VMEM((4, BLOCK, HD), F32),
            pltpu.SemaphoreType.DMA((n + 2, 4)),
        ],
        compiler_params=params(),
        name="project_block",
    )(index, *operands)


def attend_kernel(block, plan_ref, query_ref, *refs):
    keyval_refs, heads_ref = refs[:-1], refs[-1]
    scale = 1.0 / math.sqrt(HD)
    local_heads = query_ref.shape[1] // HD

    def columns_of(there, member):
        part, first = there * TILE // BLOCK, there * TILE % BLOCK
        return keyval_refs[part][member * HD : (member + 1) * HD, first : first + TILE]

    for tile in range(BLOCK // TILE):
        here = block * (BLOCK // TILE) + tile
        rows = here * TILE + lax.broadcasted_iota(jnp.int32, (TILE, 1), 0)
        begin = jnp.zeros((TILE, 1), jnp.int32)
        for s in range(8):
            begin = jnp.where(rows >= plan_ref[0, s], plan_ref[0, s], begin)
        filled = rows < plan_ref[1, 7]
        seen = []
        for there in range(max(here - 1, 0), here + 1):
            columns = there * TILE + lax.broadcasted_iota(jnp.int32, (TILE, TILE), 1)
            allowed = (columns >= begin) & (columns <= rows)
            seen.append((allowed, columns_of(there, 0), columns_of(there, 1)))
        for head in range(local_heads):
            span = slice(head * HD, (head + 1) * HD)
            query = query_ref[tile * TILE : (tile + 1) * TILE, span]
            scores = []
            for allowed, key, _ in seen:
                raw = jnp.dot(query, key, preferred_element_type=F32)
                scores.append(jnp.where(allowed, raw * scale, -1e30))
            top = functools.reduce(
                jnp.maximum, [jnp.max(s, axis=1, keepdims=True) for s in scores]
            )
            shifted = [jnp.exp(s - top) for s in scores]
            norm = sum(jnp.sum(s, axis=1, keepdims=True) for s in shifted)
            result = jnp.zeros((TILE, HD), F32)
            for part, (_, _, value) in zip(shifted, seen):
                weights = (part / norm).astype(BF)
                result += lax.dot_general(
                    weights, value, (((1,), (1,)), ((), ())), preferred_element_type=F32
                )
            heads_ref[tile * TILE : (tile + 1) * TILE, span] = jnp.where(
                filled, result, 0.0
            ).astype(BF)


def attend(block, plan, query, keyvals):
    return pl.pallas_call(
        functools.partial(attend_kernel, block),
        out_shape=jax.ShapeDtypeStruct(query.shape, BF),
        in_specs=[
            pl.BlockSpec(memory_space=pltpu.SMEM),
            pl.BlockSpec(memory_space=pltpu.VMEM),
        ]
        + [pl.BlockSpec(memory_space=pltpu.VMEM)] * len(keyvals),
        out_specs=pl.BlockSpec(memory_space=pltpu.VMEM),
        compiler_params=params(),
        name="attend",
    )(plan, query, *keyvals)


def chunks_kernel(groups, adds, index_ref, heads_ref, w_out, *refs):
    n = len(adds)
    refs = list(refs)
    weights_ref, sems = refs[-2:]
    outs = refs[-2 - len(groups) : -2]
    width = weights_ref.shape[2]
    copies = []
    for k in range(n):
        columns = pl.ds(pl.multiple_of(index_ref[k] * width, width), width)
        copies.append(
            pltpu.make_async_copy(w_out.at[:, columns], weights_ref.at[k], sems.at[k])
        )

    @pl.when(pl.program_id(0) == 0)
    def _():
        for copy in copies:
            copy.start()

    k = 0
    for out, size in zip(outs, groups):
        for j in range(size):

            @pl.when(pl.program_id(0) == 0)
            def _(k=k):
                copies[k].wait()

            total = jnp.dot(heads_ref[...], weights_ref[k], preferred_element_type=F32)
            for _ in range(adds[k]):
                total += refs.pop(0)[0].astype(F32)
            out[j] = total.astype(BF)
            k += 1


def chunks(heads, w_out, index, groups, adds, block=None, into=None):
    rows, depth = heads.shape
    width = 512
    n = len(adds)
    in_specs = [
        pl.BlockSpec((TILE, depth), lambda i, p: (i, 0)),
        pl.BlockSpec(memory_space=pltpu.HBM),
    ]
    operands = [heads, in_hbm(w_out)]
    for terms in adds:
        for array, place in terms:
            in_specs.append(
                pl.BlockSpec((1, TILE, width), lambda i, p, at=place: (at, i, 0))
            )
            operands.append(array)
    first = 0 if block is None else block * (BLOCK // TILE)
    out_rows = rows if block is None else CAP
    aliases = {}
    if into is not None:
        in_specs.append(pl.BlockSpec(memory_space=pl.ANY))
        operands.append(into)
        aliases = {len(operands): 0}
    return pl.pallas_call(
        functools.partial(chunks_kernel, groups, tuple(len(a) for a in adds)),
        input_output_aliases=aliases,
        out_shape=[jax.ShapeDtypeStruct((g, out_rows, width), BF) for g in groups],
        grid_spec=pltpu.PrefetchScalarGridSpec(
            num_scalar_prefetch=1,
            grid=(rows // TILE,),
            in_specs=in_specs,
            out_specs=[
                pl.BlockSpec((g, TILE, width), lambda i, p: (0, i + first, 0)) for g in groups
            ],
            scratch_shapes=[
                pltpu.VMEM((n, depth, width), BF),
                pltpu.SemaphoreType.DMA((n,)),
            ],
        ),
        compiler_params=params(),
        name="chunks",
    )(index, *operands)


def gather_order(x, y, c):
    way = 1 - 2 * c
    places = [(x, y, c), (x, y, 1 - c), (x, y - way, c), (x, y - way, 1 - c)]
    places += [(x, y + way, 1 - c), (x, y + way, c)]
    places += [(1 - x, y, c), (1 - x, y, 1 - c), (x, y + 2, c), (x, y + 2, 1 - c)]
    places += [(1 - x, y - way, c), (1 - x, y - way, 1 - c)]
    places += [(1 - x, y + way, 1 - c), (1 - x, y + way, c)]
    places += [(1 - x, y + 2, c), (1 - x, y + 2, 1 - c)]
    return jnp.stack(
        [side * 8 + (row + 4) % 4 * 2 + core for side, row, core in places]
    ).astype(jnp.int32)


def rotary_tables(position, member):
    lanes = jnp.arange(HD, dtype=jnp.int32)
    sign = jnp.where(lanes % 2 == 0, -1.0, 1.0).astype(F32)

    def table(pairs):
        frequency = jnp.exp(pairs.astype(F32) * (-2.0 * math.log(rope_base) / HD))
        angles = position.astype(F32)[:, None] * frequency[None, :]
        return jnp.cos(angles), jnp.sin(angles) * sign[None, :]

    q_cos, q_sin = table(lanes // 2)
    columns = member * HD + lanes
    kv_cos, kv_sin = table(columns // (2 * KVH) % (HD // 2))
    keys = member < KVH
    return q_cos, q_sin, jnp.where(keys, kv_cos, 1.0), jnp.where(keys, kv_sin, 0.0)


def body(rollout, lengths, target, w_query, w_keyval, w_out):
    member = lax.axis_index("tp")
    x, y, c = member // 8, member // 2 % 4, member % 2
    section_ids = jnp.arange(8, dtype=jnp.int32)
    own_lengths = lengths[0]
    chosen = target[0][None, :] == section_ids[:, None]
    before = jnp.cumsum(own_lengths) - own_lengths
    start_to = jnp.sum(jnp.where(chosen, before[None, :], 0), axis=1)
    sent_from = jnp.minimum(start_to // ALIGN * ALIGN, rollout.shape[0] - SENT)
    count_to = jnp.sum(jnp.where(chosen, own_lengths[None, :], 0), axis=1)
    facts = jnp.stack([count_to, start_to - sent_from], axis=1)
    outgoing = cut(rollout, sent_from)
    arrived = lax.all_to_all(outgoing, "sec", split_axis=0, concat_axis=0, tiled=True)
    facts = lax.all_to_all(facts, "sec", split_axis=0, concat_axis=0, tiled=True)
    counts, shifts = facts[:, 0], facts[:, 1]
    ends = jnp.cumsum(counts)
    offsets = ends - counts
    plan = jnp.stack([offsets, ends, shifts - offsets])
    row_ids = jnp.arange(CAP, dtype=jnp.int32)
    begin = jnp.max(
        jnp.where(row_ids[:, None] >= offsets[None, :], offsets[None, :], 0), axis=1
    )
    order = gather_order(x, y, c)
    weights = w_query[0], w_keyval[0]
    w_out = w_out[0]
    line = Line()
    way = 1 - 2 * c
    sides = (1 - x, x)

    def at(*places):
        return jnp.stack(
            [side * 8 + (row + 4) % 4 * 2 + core for side, row, core in places]
        ).astype(jnp.int32)

    def move(value, pairs):
        return send(line.next(value), pairs)

    def stack(*arrays):
        return line.add(jnp.stack([line.next(arrays[0]), *arrays[1:]]))

    def part(value, *index):
        return line.add(line.next(value)[index])

    def projected(pieces, index, *more):
        pieces = [p[None] for p in pieces]
        return line.add(project(pieces, line.next(index), *weights, *more))

    def projected_block(pieces, index, *more):
        return line.add(project_block(pieces, line.next(index), *weights, *more))

    def spread(keyval):
        keyval = lax.all_to_all(
            line.next(keyval), "tp", split_axis=0, concat_axis=0, tiled=True
        )
        return keyval.reshape(2 * HD, BLOCK)

    def attended(block, query, keyvals):
        return line.add(attend(block, line.next(plan), query, keyvals))

    def join(*arrays):
        *arrays, line.last = lax.optimization_barrier((*arrays, line.last))
        return arrays

    def summed(heads, places, groups, adds, **where):
        index = line.next(at(*places))
        return line.add(chunks(heads, w_out, index, groups, adds, **where))

    def for_core(heads, places):
        parts = summed(heads, places, (1,) * len(places), [[]] * len(places))
        return [send(p, TO_CORE) for p in parts]

    def far_for_core(heads):
        return for_core(heads, [(side, y + 2, 1 - c) for side in sides])

    def near_for_core(heads):
        places = []
        for side in sides:
            places += [(side, y - way, 1 - c), (side, y - way, c)]
        return for_core(heads, places)

    def far_sums(heads, passed):
        places = [(side, y + 2, c) for side in sides]
        adds = [[(p, 0)] for p in passed]
        return send(summed(heads, places, (2,), adds)[0], TO_Y)

    def near_sums(heads, passed, far, groups):
        places, adds = [], []
        for i, side in enumerate(sides):
            places += [(side, y + way, c), (side, y + way, 1 - c)]
            adds += [[(passed[2 * i], 0), (far, i)], [(passed[2 * i + 1], 0)]]
        return summed(heads, places, groups, adds)

    def last_sum(i, heads, near, *more, wait=None, **where):
        shared = summed(heads, [(sides[i], y, 1 - c)], (1,), [[(near, 1)]])[0]
        if wait is not None:
            near = after(near, wait)
        terms = [(t, 0) for t in (near, send(shared, TO_CORE), *more)]
        return summed(heads, [(sides[i], y, c)], (1,), [terms], **where)[0]


    value = line.add(pack(arrived, plan))
    across = send(value, TO_X)
    up = send(value, TO_Y)
    other = send(value, TO_CORE)
    up_other = send(other, TO_Y)
    position = line.next(row_ids) - begin
    tables = line.add(rotary_tables(position, member))
    total = projected([value, other, up], order[:3], CAP)
    across, up_other = join(across, up_other)
    there_up1 = [send(u[BLOCK:], TO_X) for u in (up, up_other)]
    far = send(up, TO_Y)
    across_other = send(across, TO_CORE)
    there_up0 = [send(a[:BLOCK], TO_Y) for a in (across, across_other)]
    down, down_other = send(up, TO_CORE), send(up_other, TO_CORE)
    pieces = [up_other, down, down_other, across, across_other]
    total = projected(pieces, order[3:8], CAP, total)
    far_high = after(far, total)[BLOCK:]
    far, far_high, *there_up = join(far, far_high, *there_up0, *there_up1)
    there_far0 = send(there_up[0], TO_Y)
    there_far1 = send(far_high, TO_X)
    far_other = send(far, TO_CORE)
    there_down = [send(u, TO_CORE) for u in there_up]
    pieces = [far, far_other, *there_up[:2], *there_down[:2]]
    total0 = projected_block(pieces, order[8:14], 0, total)[0]
    there_far0, far = join(there_far0, far)
    pieces = [there_far0, send(there_far0, TO_CORE)]
    index = after(order[14:], there_far1)
    query0, keyval0 = projected_block(pieces, index, 0, total0, tables)
    keyval0 = spread(keyval0)
    pieces = [far, far_other, *there_up[2:], *there_down[2:]]
    pieces += [there_far1, move(there_far1, TO_CORE)]
    query1, keyval1 = projected_block(pieces, order[8:], 1, total, tables)
    keyval1 = spread(keyval1)

    heads0 = attended(0, query0, [keyval0])
    far0 = far_sums(heads0, far_for_core(heads0))
    heads1 = attended(1, query1, [keyval0, keyval1])
    far1 = far_sums(heads1, far_for_core(heads1))
    passed = near_for_core(heads0)
    near0 = [send(t, TO_Y) for t in near_sums(heads0, passed, far0, (2, 2))]
    passed = near_for_core(heads1)
    near1 = [send(t, TO_Y) for t in near_sums(heads1, passed, far1, (2, 2))]
    crossed0 = send(last_sum(0, heads0, near0[0]), TO_X)
    crossed1 = send(last_sum(0, heads1, near1[0], wait=crossed0), TO_X)
    result = last_sum(1, heads0, near0[1], crossed0, block=0)
    return last_sum(1, heads1, near1[1], crossed1, block=1, into=result)[0]


def solution(mesh):
    placed = (
        P("sec", "tp"),
        P("sec", None),
        P("sec", None),
        P("sec", None, "tp"),
        P("sec", None, "tp"),
        P("sec", "tp", None),
    )
    return jax.shard_map(
        body, mesh=mesh, in_specs=placed, out_specs=P("sec", "tp"), check_vma=False
    )
```

```python
import functools
import math

import jax
import jax.numpy as jnp
from jax import lax
from jax.experimental import pallas as pl
from jax.experimental.pallas import tpu as pltpu
from jax.sharding import PartitionSpec as P

HQ = 64
KVH = 8
HD = 128
CAP = 1024
SLOT = 256
ALIGN = 16
SENT = SLOT + ALIGN
TILE = 256
BLOCK = 512
rope_base = 500000.0
BF = jnp.bfloat16
F32 = jnp.float32


def params():
    return pltpu.CompilerParams(vmem_limit_bytes=14 << 20)


def permutation(move):
    pairs = []
    for t in range(16):
        x, y, c = move(t // 8, t // 2 % 4, t % 2)
        pairs.append((t, x % 2 * 8 + y % 4 * 2 + c % 2))
    return pairs


TO_CORE = permutation(lambda x, y, c: (x, y, c + 1))
TO_X = permutation(lambda x, y, c: (x + 1, y, c))
TO_Y = permutation(lambda x, y, c: (x, y + 1 - 2 * c, c))


def after(value, *others):
    return lax.optimization_barrier((value, *others))[0]


class Line:
    def __init__(self):
        self.last = None

    def next(self, value):
        return value if self.last is None else after(value, self.last)

    def add(self, result):
        self.last = jax.tree.leaves(result)[0]
        return result


def send(value, pairs):
    return lax.ppermute(value, "tp", pairs)


def in_hbm(array):
    return pltpu.with_memory_space_constraint(array, pltpu.HBM)


def cut_kernel(start_ref, rollout_ref, sent_ref):
    for d in range(8):
        row = pl.multiple_of(start_ref[d], ALIGN)
        sent_ref[d] = rollout_ref[pl.ds(row, SENT), :]


def cut(rollout, starts):
    return pl.pallas_call(
        cut_kernel,
        out_shape=jax.ShapeDtypeStruct((8, SENT, rollout.shape[1]), BF),
        in_specs=[
            pl.BlockSpec(memory_space=pltpu.SMEM),
            pl.BlockSpec(memory_space=pltpu.VMEM),
        ],
        out_specs=pl.BlockSpec(memory_space=pltpu.VMEM),
        compiler_params=params(),
        name="cut",
    )(starts, rollout)


def pack_kernel(plan_ref, arrived_ref, packed_ref, total_ref):
    first = pl.program_id(0) * TILE
    rows = first + lax.broadcasted_iota(jnp.int32, (TILE, 1), 0)
    slots = lax.broadcasted_iota(jnp.int32, (TILE, SENT), 1)
    total_ref[...] = jnp.zeros_like(total_ref)

    @pl.loop(0, 8)
    def _(s):
        begin, end = plan_ref[0, s], plan_ref[1, s]

        @pl.when((begin < first + TILE) & (end > first))
        def _():
            source = jnp.where(
                (rows >= begin) & (rows < end), rows + plan_ref[2, s], -1
            )
            picked = jnp.where(slots == source, 1.0, 0.0).astype(BF)
            total_ref[...] += jnp.dot(
                picked, arrived_ref[s], preferred_element_type=F32
            )

    packed_ref[...] = total_ref[...].astype(BF)


def pack(arrived, plan):
    width = arrived.shape[2]
    return pl.pallas_call(
        pack_kernel,
        out_shape=jax.ShapeDtypeStruct((CAP, width), BF),
        grid_spec=pltpu.PrefetchScalarGridSpec(
            num_scalar_prefetch=1,
            grid=(CAP // TILE,),
            in_specs=[pl.BlockSpec(memory_space=pltpu.VMEM)],
            out_specs=pl.BlockSpec((TILE, width), lambda i, p: (i, 0)),
            scratch_shapes=[pltpu.VMEM((TILE, width), F32)],
        ),
        compiler_params=params(),
        name="pack",
    )(plan, arrived)


def swap_members(values):
    lanes = lax.broadcasted_iota(jnp.int32, values.shape, 1)
    return jnp.where(
        lanes % 2 == 0, pltpu.roll(values, HD - 1, 1), pltpu.roll(values, 1, 1)
    )


def heads_first(keyval):
    to = lax.broadcasted_iota(jnp.int32, (HD, HD), 0)
    came = lax.broadcasted_iota(jnp.int32, (HD, HD), 1)
    order = jnp.where(came == to % 16 // 2 * 16 + to // 16 * 2 + to % 2, 1.0, 0.0).astype(BF)
    return lax.dot_general(
        order, keyval, (((1,), (1,)), ((), ())), preferred_element_type=F32
    ).astype(BF)


def project_kernel(counts, has_total, last, index_ref, *refs):
    refs = list(refs)
    pieces = [refs.pop(0) for _ in counts]
    query_w, keyval_w = refs.pop(0), refs.pop(0)
    total_ref = refs.pop(0) if has_total else None
    tables = [refs.pop(0) for _ in range(4)] if last else None
    weights_ref, sems = refs[-2:]
    refs = refs[:-2]
    columns = query_w.shape[1]
    depth = pieces[0].shape[2]
    copies = []
    for k in range(sum(counts)):
        rows = pl.ds(pl.multiple_of(index_ref[k] * depth, depth), depth)
        copies.append((
            pltpu.make_async_copy(
                query_w.at[rows, :], weights_ref.at[k, :, pl.ds(0, columns)], sems.at[k, 0]
            ),
            pltpu.make_async_copy(
                keyval_w.at[rows, :], weights_ref.at[k, :, pl.ds(columns, HD)], sems.at[k, 1]
            ),
        ))

    @pl.when(pl.program_id(0) == 0)
    def _():
        for pair in copies:
            for copy in pair:
                copy.start()

    query = total_ref[:, :columns] if has_total else 0.0
    keyval = total_ref[:, columns:] if has_total else 0.0
    k = 0
    for ref, count in zip(pieces, counts):
        for j in range(count):

            @pl.when(pl.program_id(0) == 0)
            def _(k=k):
                for copy in copies[k]:
                    copy.wait()

            left = ref[j]
            query += jnp.dot(left, weights_ref[k, :, :columns], preferred_element_type=F32)
            keyval += jnp.dot(left, weights_ref[k, :, columns:], preferred_element_type=F32)
            k += 1
    if not last:
        refs[0][:, :columns] = query
        refs[0][:, columns:] = keyval
        return
    query_out, keyval_out = refs
    q_cos, q_sin, kv_cos, kv_sin = [t[...] for t in tables]
    for head in range(columns // HD):
        span = slice(head * HD, (head + 1) * HD)
        part = query[:, span]
        query_out[:, span] = (part * q_cos + swap_members(part) * q_sin).astype(BF)
    turned = (keyval * kv_cos + swap_members(keyval) * kv_sin).astype(BF)
    turned = heads_first(turned)
    for member in range(2 * KVH):
        keyval_out[member] = turned[member // 2 * 16 : member // 2 * 16 + 16]


def project(pieces, index, w_query, w_keyval, rows, total=None, tables=None, block=0):
    counts = tuple(p.shape[0] for p in pieces)
    n = sum(counts)
    width = pieces[0].shape[2]
    columns = w_query.shape[1]
    last = tables is not None

    def skip(array, axis):
        return block * (BLOCK // TILE) if array.shape[axis] > rows else 0

    in_specs = [
        pl.BlockSpec((p.shape[0], TILE, width), lambda i, _, at=skip(p, 1): (0, i + at, 0))
        for p in pieces
    ]
    in_specs += [pl.BlockSpec(memory_space=pltpu.HBM)] * 2
    operands = list(pieces) + [in_hbm(w_query), in_hbm(w_keyval)]
    if total is not None:
        at = skip(total, 0)
        in_specs.append(pl.BlockSpec((TILE, columns + HD), lambda i, _: (i + at, 0)))
        operands.append(in_hbm(total))
    if last:
        first = skip(tables[0], 0)
        in_specs += [pl.BlockSpec((TILE, HD), lambda i, _: (i + first, 0))] * 4
        operands += [in_hbm(t) for t in tables]
        out_shape = (
            jax.ShapeDtypeStruct((rows, columns), BF),
            jax.ShapeDtypeStruct((2 * KVH, 16, rows), BF),
        )
        out_specs = [
            pl.BlockSpec((TILE, columns), lambda i, _: (i, 0)),
            pl.BlockSpec((2 * KVH, 16, TILE), lambda i, _: (0, 0, i)),
        ]
    else:
        out_shape = jax.ShapeDtypeStruct((rows, columns + HD), F32)
        out_specs = pl.BlockSpec((TILE, columns + HD), lambda i, _: (i, 0))
    return pl.pallas_call(
        functools.partial(project_kernel, counts, total is not None, last),
        out_shape=out_shape,
        grid_spec=pltpu.PrefetchScalarGridSpec(
            num_scalar_prefetch=1,
            grid=(rows // TILE,),
            in_specs=in_specs,
            out_specs=out_specs,
            scratch_shapes=[
                pltpu.VMEM((n, width, columns + HD), BF),
                pltpu.SemaphoreType.DMA((n, 2)),
            ],
        ),
        compiler_params=params(),
        name="project",
    )(index, *operands)


def project_block_kernel(skips, last, index_ref, *refs):
    refs = list(refs)
    n = len(skips) - 2
    pieces = [refs.pop(0) for _ in range(n)]
    query_w, keyval_w, total = refs.pop(0), refs.pop(0), refs.pop(0)
    tables = [refs.pop(0) for _ in range(4)] if last else []
    *outs, left_ref, weights_ref, sum_ref, table_ref, sems = refs
    depth, columns = left_ref.shape[2], query_w.shape[1]
    copy = pltpu.make_async_copy
    fetches = []
    for k, piece in enumerate(pieces):
        rows = pl.ds(pl.multiple_of(index_ref[k] * depth, depth), depth)
        fetches.append([
            copy(piece.at[pl.ds(skips[k], BLOCK), :], left_ref.at[k], sems.at[k, 0]),
            copy(query_w.at[rows, :], weights_ref.at[k, :, pl.ds(0, columns)], sems.at[k, 1]),
            copy(keyval_w.at[rows, :], weights_ref.at[k, :, pl.ds(columns, HD)], sems.at[k, 2]),
        ])
    fetch_total = copy(total.at[pl.ds(skips[n], BLOCK), :], sum_ref, sems.at[n, 0])
    fetch_tables = [
        copy(table.at[pl.ds(skips[n + 1], BLOCK), :], table_ref.at[j], sems.at[n + 1, j])
        for j, table in enumerate(tables)
    ]
    for fetch in [*fetches[0], fetch_total, *sum(fetches[1:], []), *fetch_tables]:
        fetch.start()
    for k in range(n):
        for fetch in fetches[k]:
            fetch.wait()
        if k == 0:
            fetch_total.wait()
        for tile in range(BLOCK // TILE):
            rows = slice(tile * TILE, (tile + 1) * TILE)
            left = left_ref[k, rows, :]
            for span in (slice(0, columns), slice(columns, columns + HD)):
                sum_ref[rows, span] += jnp.dot(
                    left, weights_ref[k, :, span], preferred_element_type=F32
                )
    for fetch in fetch_tables:
        fetch.wait()
    if not last:
        outs[0][...] = sum_ref[...]
        return
    query_out, keyval_out = outs
    for tile in range(BLOCK // TILE):
        rows = slice(tile * TILE, (tile + 1) * TILE)
        q_cos, q_sin, kv_cos, kv_sin = [table_ref[j, rows, :] for j in range(4)]
        for head in range(columns // HD):
            span = slice(head * HD, (head + 1) * HD)
            part = sum_ref[rows, span]
            query_out[rows, span] = (part * q_cos + swap_members(part) * q_sin).astype(BF)
        part = sum_ref[rows, columns:]
        turned = heads_first((part * kv_cos + swap_members(part) * kv_sin).astype(BF))
        for member in range(2 * KVH):
            keyval_out[member, :, rows] = turned[member // 2 * 16 : member // 2 * 16 + 16]


def project_block(pieces, index, w_query, w_keyval, block, total, tables=()):
    n = len(pieces)
    width, columns = pieces[0].shape[1], w_query.shape[1]
    last = len(tables) > 0
    skips = [
        block * BLOCK if a.shape[0] > BLOCK else 0 for a in (*pieces, total, *tables[:1])
    ]
    if not last:
        skips.append(0)
    operands = [in_hbm(a) for a in (*pieces, w_query, w_keyval, total, *tables)]
    if last:
        out_shape = (
            jax.ShapeDtypeStruct((BLOCK, columns), BF),
            jax.ShapeDtypeStruct((2 * KVH, 16, BLOCK), BF),
        )
    else:
        out_shape = (jax.ShapeDtypeStruct((BLOCK, columns + HD), F32),)
    return pl.pallas_call(
        functools.partial(project_block_kernel, tuple(skips), last),
        out_shape=out_shape,
        in_specs=[pl.BlockSpec(memory_space=pltpu.SMEM)]
        + [pl.BlockSpec(memory_space=pltpu.HBM)] * len(operands),
        out_specs=[pl.BlockSpec(memory_space=pltpu.VMEM)] * len(out_shape),
        scratch_shapes=[
            pltpu.VMEM((n, BLOCK, width), BF),
            pltpu.VMEM((n, width, columns + HD), BF),
            pltpu.VMEM((BLOCK, columns + HD), F32),
            pltpu.VMEM((4, BLOCK, HD), F32),
            pltpu.SemaphoreType.DMA((n + 2, 4)),
        ],
        compiler_params=params(),
        name="project_block",
    )(index, *operands)


def attend_kernel(block, plan_ref, query_ref, *refs):
    keyval_refs, heads_ref = refs[:-1], refs[-1]
    scale = 1.0 / math.sqrt(HD)
    local_heads = query_ref.shape[1] // HD

    def columns_of(there, member):
        part, first = there * TILE // BLOCK, there * TILE % BLOCK
        return keyval_refs[part][member * HD : (member + 1) * HD, first : first + TILE]

    for tile in range(BLOCK // TILE):
        here = block * (BLOCK // TILE) + tile
        rows = here * TILE + lax.broadcasted_iota(jnp.int32, (TILE, 1), 0)
        begin = jnp.zeros((TILE, 1), jnp.int32)
        for s in range(8):
            begin = jnp.where(rows >= plan_ref[0, s], plan_ref[0, s], begin)
        filled = rows < plan_ref[1, 7]
        seen = []
        for there in range(max(here - 1, 0), here + 1):
            columns = there * TILE + lax.broadcasted_iota(jnp.int32, (TILE, TILE), 1)
            allowed = (columns >= begin) & (columns <= rows)
            seen.append((allowed, columns_of(there, 0), columns_of(there, 1)))
        for head in range(local_heads):
            span = slice(head * HD, (head + 1) * HD)
            query = query_ref[tile * TILE : (tile + 1) * TILE, span]
            scores = []
            for allowed, key, _ in seen:
                raw = jnp.dot(query, key, preferred_element_type=F32)
                scores.append(jnp.where(allowed, raw * scale, -1e30))
            top = functools.reduce(
                jnp.maximum, [jnp.max(s, axis=1, keepdims=True) for s in scores]
            )
            shifted = [jnp.exp(s - top) for s in scores]
            norm = sum(jnp.sum(s, axis=1, keepdims=True) for s in shifted)
            result = jnp.zeros((TILE, HD), F32)
            for part, (_, _, value) in zip(shifted, seen):
                weights = (part / norm).astype(BF)
                result += lax.dot_general(
                    weights, value, (((1,), (1,)), ((), ())), preferred_element_type=F32
                )
            heads_ref[tile * TILE : (tile + 1) * TILE, span] = jnp.where(
                filled, result, 0.0
            ).astype(BF)


def attend(block, plan, query, keyvals):
    return pl.pallas_call(
        functools.partial(attend_kernel, block),
        out_shape=jax.ShapeDtypeStruct(query.shape, BF),
        in_specs=[
            pl.BlockSpec(memory_space=pltpu.SMEM),
            pl.BlockSpec(memory_space=pltpu.VMEM),
        ]
        + [pl.BlockSpec(memory_space=pltpu.VMEM)] * len(keyvals),
        out_specs=pl.BlockSpec(memory_space=pltpu.VMEM),
        compiler_params=params(),
        name="attend",
    )(plan, query, *keyvals)


def chunks_kernel(groups, adds, index_ref, heads_ref, w_out, *refs):
    n = len(adds)
    refs = list(refs)
    weights_ref, sems = refs[-2:]
    outs = refs[-2 - len(groups) : -2]
    width = weights_ref.shape[2]
    copies = []
    for k in range(n):
        columns = pl.ds(pl.multiple_of(index_ref[k] * width, width), width)
        copies.append(
            pltpu.make_async_copy(w_out.at[:, columns], weights_ref.at[k], sems.at[k])
        )

    @pl.when(pl.program_id(0) == 0)
    def _():
        for copy in copies:
            copy.start()

    k = 0
    for out, size in zip(outs, groups):
        for j in range(size):

            @pl.when(pl.program_id(0) == 0)
            def _(k=k):
                copies[k].wait()

            total = jnp.dot(heads_ref[...], weights_ref[k], preferred_element_type=F32)
            for _ in range(adds[k]):
                total += refs.pop(0)[0].astype(F32)
            out[j] = total.astype(BF)
            k += 1


def chunks(heads, w_out, index, groups, adds, block=None, into=None):
    rows, depth = heads.shape
    width = 512
    n = len(adds)
    in_specs = [
        pl.BlockSpec((TILE, depth), lambda i, p: (i, 0)),
        pl.BlockSpec(memory_space=pltpu.HBM),
    ]
    operands = [heads, in_hbm(w_out)]
    for terms in adds:
        for array, place in terms:
            in_specs.append(
                pl.BlockSpec((1, TILE, width), lambda i, p, at=place: (at, i, 0))
            )
            operands.append(array)
    first = 0 if block is None else block * (BLOCK // TILE)
    out_rows = rows if block is None else CAP
    aliases = {}
    if into is not None:
        in_specs.append(pl.BlockSpec(memory_space=pl.ANY))
        operands.append(into)
        aliases = {len(operands): 0}
    return pl.pallas_call(
        functools.partial(chunks_kernel, groups, tuple(len(a) for a in adds)),
        input_output_aliases=aliases,
        out_shape=[jax.ShapeDtypeStruct((g, out_rows, width), BF) for g in groups],
        grid_spec=pltpu.PrefetchScalarGridSpec(
            num_scalar_prefetch=1,
            grid=(rows // TILE,),
            in_specs=in_specs,
            out_specs=[
                pl.BlockSpec((g, TILE, width), lambda i, p: (0, i + first, 0)) for g in groups
            ],
            scratch_shapes=[
                pltpu.VMEM((n, depth, width), BF),
                pltpu.SemaphoreType.DMA((n,)),
            ],
        ),
        compiler_params=params(),
        name="chunks",
    )(index, *operands)


def gather_order(x, y, c):
    way = 1 - 2 * c
    places = [(x, y, c), (x, y, 1 - c), (x, y - way, c), (x, y - way, 1 - c)]
    places += [(x, y + way, 1 - c), (x, y + way, c)]
    places += [(1 - x, y, c), (1 - x, y, 1 - c), (x, y + 2, c), (x, y + 2, 1 - c)]
    places += [(1 - x, y - way, c), (1 - x, y - way, 1 - c)]
    places += [(1 - x, y + way, 1 - c), (1 - x, y + way, c)]
    places += [(1 - x, y + 2, c), (1 - x, y + 2, 1 - c)]
    return jnp.stack(
        [side * 8 + (row + 4) % 4 * 2 + core for side, row, core in places]
    ).astype(jnp.int32)


def rotary_tables(position, member):
    lanes = jnp.arange(HD, dtype=jnp.int32)
    sign = jnp.where(lanes % 2 == 0, -1.0, 1.0).astype(F32)

    def table(pairs):
        frequency = jnp.exp(pairs.astype(F32) * (-2.0 * math.log(rope_base) / HD))
        angles = position.astype(F32)[:, None] * frequency[None, :]
        return jnp.cos(angles), jnp.sin(angles) * sign[None, :]

    q_cos, q_sin = table(lanes // 2)
    columns = member * HD + lanes
    kv_cos, kv_sin = table(columns // (2 * KVH) % (HD // 2))
    keys = member < KVH
    return q_cos, q_sin, jnp.where(keys, kv_cos, 1.0), jnp.where(keys, kv_sin, 0.0)


def body(rollout, lengths, target, w_query, w_keyval, w_out):
    member = lax.axis_index("tp")
    x, y, c = member // 8, member // 2 % 4, member % 2
    section_ids = jnp.arange(8, dtype=jnp.int32)
    own_lengths = lengths[0]
    chosen = target[0][None, :] == section_ids[:, None]
    before = jnp.cumsum(own_lengths) - own_lengths
    start_to = jnp.sum(jnp.where(chosen, before[None, :], 0), axis=1)
    sent_from = jnp.minimum(start_to // ALIGN * ALIGN, rollout.shape[0] - SENT)
    count_to = jnp.sum(jnp.where(chosen, own_lengths[None, :], 0), axis=1)
    facts = jnp.stack([count_to, start_to - sent_from], axis=1)
    outgoing = cut(rollout, sent_from)
    arrived = lax.all_to_all(outgoing, "sec", split_axis=0, concat_axis=0, tiled=True)
    facts = lax.all_to_all(facts, "sec", split_axis=0, concat_axis=0, tiled=True)
    counts, shifts = facts[:, 0], facts[:, 1]
    ends = jnp.cumsum(counts)
    offsets = ends - counts
    plan = jnp.stack([offsets, ends, shifts - offsets])
    row_ids = jnp.arange(CAP, dtype=jnp.int32)
    begin = jnp.max(
        jnp.where(row_ids[:, None] >= offsets[None, :], offsets[None, :], 0), axis=1
    )
    order = gather_order(x, y, c)
    weights = w_query[0], w_keyval[0]
    w_out = w_out[0]
    line = Line()
    way = 1 - 2 * c
    sides = (1 - x, x)

    def at(*places):
        return jnp.stack(
            [side * 8 + (row + 4) % 4 * 2 + core for side, row, core in places]
        ).astype(jnp.int32)

    def move(value, pairs):
        return send(line.next(value), pairs)

    def stack(*arrays):
        return line.add(jnp.stack([line.next(arrays[0]), *arrays[1:]]))

    def part(value, *index):
        return line.add(line.next(value)[index])

    def projected(pieces, index, *more):
        pieces = [p[None] for p in pieces]
        return line.add(project(pieces, line.next(index), *weights, *more))

    def projected_block(pieces, index, *more):
        return line.add(project_block(pieces, line.next(index), *weights, *more))

    def spread(keyval):
        keyval = lax.all_to_all(
            line.next(keyval), "tp", split_axis=0, concat_axis=0, tiled=True
        )
        return keyval.reshape(2 * HD, BLOCK)

    def attended(block, query, keyvals):
        return line.add(attend(block, line.next(plan), query, keyvals))

    def join(*arrays):
        *arrays, line.last = lax.optimization_barrier((*arrays, line.last))
        return arrays

    def summed(heads, places, groups, adds, **where):
        index = line.next(at(*places))
        return line.add(chunks(heads, w_out, index, groups, adds, **where))

    def for_core(heads, places):
        parts = summed(heads, places, (1,) * len(places), [[]] * len(places))
        return [send(p, TO_CORE) for p in parts]

    def far_for_core(heads):
        return for_core(heads, [(side, y + 2, 1 - c) for side in sides])

    def near_for_core(heads):
        places = []
        for side in sides:
            places += [(side, y - way, 1 - c), (side, y - way, c)]
        return for_core(heads, places)

    def far_sums(heads, passed):
        places = [(side, y + 2, c) for side in sides]
        adds = [[(p, 0)] for p in passed]
        return send(summed(heads, places, (2,), adds)[0], TO_Y)

    def near_sums(heads, passed, far, groups):
        places, adds = [], []
        for i, side in enumerate(sides):
            places += [(side, y + way, c), (side, y + way, 1 - c)]
            adds += [[(passed[2 * i], 0), (far, i)], [(passed[2 * i + 1], 0)]]
        return summed(heads, places, groups, adds)

    def last_sum(i, heads, near, *more, wait=None, **where):
        shared = summed(heads, [(sides[i], y, 1 - c)], (1,), [[(near, 1)]])[0]
        if wait is not None:
            near = after(near, wait)
        terms = [(t, 0) for t in (near, send(shared, TO_CORE), *more)]
        return summed(heads, [(sides[i], y, c)], (1,), [terms], **where)[0]


    value = line.add(pack(arrived, plan))
    across = send(value, TO_X)
    up = send(value, TO_Y)
    other = send(value, TO_CORE)
    up_other = send(other, TO_Y)
    position = line.next(row_ids) - begin
    tables = line.add(rotary_tables(position, member))
    total = projected([value, other, up], order[:3], CAP)
    across, up_other = join(across, up_other)
    there_up1 = [send(u[BLOCK:], TO_X) for u in (up, up_other)]
    far = send(up, TO_Y)
    across_other = send(across, TO_CORE)
    there_up0 = [send(a[:BLOCK], TO_Y) for a in (across, across_other)]
    down, down_other = send(up, TO_CORE), send(up_other, TO_CORE)
    pieces = [up_other, down, down_other, across, across_other]
    total = projected(pieces, order[3:8], CAP, total)
    far_high = after(far, total)[BLOCK:]
    far, far_high, *there_up = join(far, far_high, *there_up0, *there_up1)
    there_far0 = send(there_up[0], TO_Y)
    there_far1 = send(far_high, TO_X)
    far_other = send(far, TO_CORE)
    there_down = [send(u, TO_CORE) for u in there_up]
    pieces = [far, far_other, *there_up[:2], *there_down[:2]]
    total0 = projected_block(pieces, order[8:14], 0, total)[0]
    there_far0, far = join(there_far0, far)
    pieces = [there_far0, send(there_far0, TO_CORE)]
    query0, keyval0 = projected_block(pieces, order[14:], 0, total0, tables)
    keyval0 = spread(after(keyval0, there_far1))
    pieces = [far, far_other, *there_up[2:], *there_down[2:]]
    pieces += [there_far1, move(there_far1, TO_CORE)]
    query1, keyval1 = projected_block(pieces, order[8:], 1, total, tables)
    keyval1 = spread(keyval1)

    heads0 = attended(0, query0, [keyval0])
    far0 = far_sums(heads0, far_for_core(heads0))
    heads1 = attended(1, query1, [keyval0, keyval1])
    far1 = far_sums(heads1, far_for_core(heads1))
    passed = near_for_core(heads0)
    near0 = [send(t, TO_Y) for t in near_sums(heads0, passed, far0, (2, 2))]
    passed = near_for_core(heads1)
    near1 = [send(t, TO_Y) for t in near_sums(heads1, passed, far1, (2, 2))]
    crossed0 = send(last_sum(0, heads0, near0[0]), TO_X)
    crossed1 = send(last_sum(0, heads1, near1[0], wait=crossed0), TO_X)
    result = last_sum(1, heads0, near0[1], crossed0, block=0)
    return last_sum(1, heads1, near1[1], crossed1, block=1, into=result)[0]


def solution(mesh):
    placed = (
        P("sec", "tp"),
        P("sec", None),
        P("sec", None),
        P("sec", None, "tp"),
        P("sec", None, "tp"),
        P("sec", "tp", None),
    )
    return jax.shard_map(
        body, mesh=mesh, in_specs=placed, out_specs=P("sec", "tp"), check_vma=False
    )
```
